512 devices in a mesh: leaf: 4 (over y_hi, core), row: 4 (over x), col: 32 (over y_lo, z).
Axes of the slice: x: 4, y: 8 (y_hi: 2, y_lo: 4; y = y_hi * 4 + y_lo), z: 8, core: 2. Of those that a mesh axis runs over, the one named last changes fastest.
Arguments:
- root_inverse: bfloat16 [4096, 4096], P('col', ('leaf', 'row')), as said below
- factor_first: bfloat16 [2, 4096, 2048], P(None, 'col', 'row'), may hold values from -0.09375 to 0.09375
- local_first: bfloat16 [2, 2048, 2048], P(None, 'col', 'row'), as said below
- factor_second: bfloat16 [4, 4096, 1536], P('leaf', 'col', 'row'), may hold values from -0.09375 to 0.09375
- local_second: float32 [4, 1536], P('leaf', 'row'), may hold values from 0.5 to 2
- ancestor_map: int32 [4, 16], replicated, may hold values from 0 to 31, as said below
Outputs:
- variance: float32 [4, 1536], P('leaf', 'row')
The draws below stay inside these ranges and needn't reach their ends.
Inputs may be any that keep to these rules, and one draw needn't show every extreme that they name: `ancestor_map`: each row lists 16 different root blocks; some row names block 0 and some row names block 31. `root_inverse`: Symmetric. `local_first`: symmetric in its last two dimensions.
All inputs are finite; a program needn't handle non-finite values.
Results may differ from the reference program's by a relative error of at most 0.0003.
Values may be sent and summed in bfloat16 or wider, within the bound.
A program may use at most 64 MiB of HBM per device.

```python
import math
import jax
import jax.numpy as jnp
from jax import lax

BLK = 128
NBR = 32
S1 = 2048
K2 = 16
S2 = 1536
R = 4096
ANC2 = 2048


def symmetric_noise(noise, width):
    return (noise + jnp.swapaxes(noise, -1, -2)) * (0.25 / math.sqrt(width))


def draw_root_inverse(key, part):
    key = jax.random.fold_in(key, 11)
    first_key, second_key = jax.random.split(key)
    noise = jax.random.normal(first_key, (R, R), jnp.float32)
    diagonal = jnp.exp(jax.random.uniform(second_key, (R,), jnp.float32, 0.0, 1.1))
    matrix = symmetric_noise(noise, R) + jnp.eye(R, dtype=jnp.float32) * diagonal[None, :]
    return matrix.astype(jnp.bfloat16)


def draw_local_first(key, part):
    key = jax.random.fold_in(key, 12)
    first_key, second_key = jax.random.split(key)
    noise = jax.random.normal(first_key, (2, S1, S1), jnp.float32)
    diagonal = jnp.exp(jax.random.uniform(second_key, (2, S1), jnp.float32, 0.0, 1.1))
    matrix = symmetric_noise(noise, S1) + jnp.eye(S1, dtype=jnp.float32)[None, :, :] * diagonal[:, None, :]
    return matrix.astype(jnp.bfloat16)


def draw_ancestor_map(key, part):
    key = jax.random.fold_in(key, 13)
    row_keys = jax.random.split(key, 4)
    listing = []
    for number in range(4):
        order = jax.random.permutation(row_keys[number], NBR).astype(jnp.int32)
        wanted = NBR - 1 if number == 0 else 0
        place = jnp.argmax(order == wanted)
        order = order.at[place].set(order[0]).at[0].set(wanted)
        listing.append(order[:K2])
    return jnp.stack(listing).astype(jnp.int32)


def block_levels(rng, shape, cuts, smallest, high):
    loudness = 1.0
    for axis_at, shards_of in cuts:
        heights = jax.random.uniform(jax.random.fold_in(jax.random.fold_in(rng, 6), axis_at), (shards_of,), jnp.float32, smallest / len(cuts), high / len(cuts))
        loudness = loudness * jnp.repeat(jnp.exp(heights), shape[axis_at] // shards_of).reshape((-1,) + (1,) * (len(shape) - 1 - axis_at))
    return loudness


def centred(key, dims, scale, bound, cuts=(), kind=jnp.bfloat16):
    factor_of = block_levels(key, dims, cuts, -0.22, 0.18) if cuts else 1.0
    entries = jax.random.normal(key, dims, jnp.float32) * scale * factor_of
    return jnp.minimum(jnp.maximum(entries, -bound), bound).astype(kind)


def setup_inputs(seed: int = 0) -> dict:
    keys = jax.random.split(jax.random.key(seed), 7)
    return {
        "root_inverse": draw_root_inverse(jax.random.fold_in(keys[6], 71), 0),
        "factor_first": centred(keys[1], (2, R, S1), R ** -0.5, 0.09375, ((1, 32), (2, 4))),
        "local_first": draw_local_first(jax.random.fold_in(keys[6], 71), 0),
        "factor_second": centred(keys[3], (4, ANC2 + S1, S2), (ANC2 + S1) ** -0.5, 0.09375, ((0, 4), (1, 32), (2, 4))),
        "local_second": jnp.clip(jnp.exp(math.log(2.0) - 1.3862944 * jax.random.uniform(keys[4], (4, S2), jnp.float32) ** block_levels(keys[4], (4, S2), ((0, 4), (1, 4)), -0.2, 0.2)), 0.5, 2.0),
        "ancestor_map": draw_ancestor_map(jax.random.fold_in(keys[6], 71), 0),
    }


def reference(root_inverse, factor_first, local_first, factor_second, local_second, ancestor_map):
    highest = lax.Precision.HIGHEST
    cross_list = []
    parent_list = []
    for parent in range(2):
        factor = factor_first[parent]
        cross_block = jnp.dot(root_inverse, factor, preferred_element_type=jnp.float32)
        parent_inv = local_first[parent].astype(jnp.float32) + jnp.dot(factor.astype(jnp.float32).T, cross_block, precision=highest)
        cross_list.append(cross_block)
        parent_list.append(parent_inv)
    results = []
    for subtree in range(4):
        parent = subtree // 2
        second = factor_second[subtree]
        root_part = second[:ANC2]
        parent_part = second[ANC2:].astype(jnp.float32)
        row_ids = (ancestor_map[subtree][:, None] * BLK + jnp.arange(BLK, dtype=jnp.int32)[None, :]).reshape(-1).astype(jnp.int32)
        padded = jnp.zeros((R, S2), jnp.bfloat16).at[row_ids].set(root_part)
        root_term = jnp.dot(root_inverse, padded, preferred_element_type=jnp.float32)
        cross_term = jnp.dot(cross_list[parent], parent_part, precision=highest)
        parent_term = jnp.dot(parent_list[parent], parent_part, precision=highest)
        variance = local_second[subtree] + jnp.sum(padded.astype(jnp.float32) * (root_term - 2.0 * cross_term), 0) + jnp.sum(parent_part * parent_term, 0)
        results.append(variance)
    return jnp.stack(results)
```

```python
import jax
import jax.numpy as jnp
from jax import lax
from jax.experimental import pallas as pl
from jax.experimental.pallas import tpu as pltpu
from jax.sharding import PartitionSpec as P

NX, NU, NZ = 4, 4, 8
BLK = 128
SUB = 96
SLOTS = 16
MESH = pl.DeviceIdType.MESH
BF16, F32 = jnp.bfloat16, jnp.float32
NT = (((1,), (1,)), ((), ()))


def dot_nt(a, b):
    return lax.dot_general(a, b, NT, preferred_element_type=F32)


def kernel(
    r_ref, f_ref, l_ref, v_ref, loc_ref, map_ref, out_ref,
    vs, vall, fg, lg, rg, wk, wm, acc, sums, red1, red2,
    own_sem, vsc_s, vsc_r, vz_s, vz_r, fy_s, fy_r, fx_s, fx_r, fd_s, fd_r,
    ly_s, ly_r, lx_s, lx_r, ld_s, ld_r, ry_s, ry_r, rx_s, rx_r, rd_s, rd_r,
    wc_s, wc_r, wf_s, wf_r, wz_s, wz_r, d1_s, d1_r, d2_s, d2_r,
):
    leaf, x, col = lax.axis_index("leaf"), lax.axis_index("row"), lax.axis_index("col")
    h, c = lax.div(leaf, 2), lax.rem(leaf, 2)
    u, z = lax.div(col, NZ), lax.rem(col, NZ)
    y = h * NU + u
    sgn = 1 - 2 * c

    def at_z(zz):
        return (leaf, x, u * NZ + zz)

    def at_u(uu):
        return (leaf, x, uu * NZ + z)

    def at_x(xx):
        return (leaf, xx, col)

    def at_y(yy, core):
        return (lax.div(yy, NU) * 2 + core, x, lax.rem(yy, NU) * NZ + z)

    def zmod(v):
        return lax.rem(v + 2 * NZ, NZ)

    def xmod(v):
        return lax.rem(v + 2 * NX, NX)

    def umod(v):
        return lax.rem(v + 2 * NU, NU)

    started = []

    def send(src, dst, ssem, rsem, to):
        copy = pltpu.make_async_remote_copy(
            src_ref=src, dst_ref=dst, send_sem=ssem, recv_sem=rsem, device_id=to, device_id_type=MESH
        )
        copy.start()
        started.append(copy)

    def arrived(dst, rsem):
        pltpu.make_async_remote_copy(
            src_ref=dst, dst_ref=dst, send_sem=rsem, recv_sem=rsem, device_id=at_z(zmod(z + 1)), device_id_type=MESH
        ).wait_recv()

    barrier = pltpu.get_barrier_semaphore()
    peers = []
    for d in range(1, 16):
        number = lax.rem(y * 2 + c + d, 16)
        peers.append(at_y(lax.div(number, 2), lax.rem(number, 2)))
    peers += [at_z(zmod(z + d)) for d in range(1, NZ)]
    peers += [at_x(xmod(x + 1)), at_x(xmod(x - 1))]
    for peer in peers:
        pl.semaphore_signal(barrier, inc=1, device_id=peer, device_id_type=MESH)

    half = pl.ds(pl.multiple_of(c * 64, 64), 64)
    quarter = pl.ds(pl.multiple_of(c * 32, 32), 32)
    own_f = pltpu.make_async_copy(f_ref.at[h, half], fg.at[x, u, c], own_sem.at[0])
    own_l = pltpu.make_async_copy(l_ref.at[h, quarter], lg.at[x, u, c], own_sem.at[1])
    own_f.start()
    own_l.start()
    vt = jnp.transpose(v_ref[0].astype(F32)).astype(BF16)
    vs[...] = vt.reshape(NU, SUB, BLK)
    vall[z, u] = vs[u]
    own_f.wait()
    own_l.wait()
    pl.semaphore_wait(barrier, len(peers))

    for d in range(1, NU):
        to = umod(u + d)
        send(vs.at[to], vall.at[z, u], vsc_s.at[d], vsc_r.at[d], at_u(to))
    xa, xb = xmod(x + sgn), xmod(x - sgn)
    y_steps = [sgn, -sgn, 2 * sgn]
    for i, step in enumerate(y_steps):
        yy = lax.rem(y + step + 16, 8)
        send(f_ref.at[lax.div(yy, NU), half], fg.at[x, u, c], fy_s.at[i], fy_r.at[i], at_y(yy, c))
    u_from = [u] + [umod(u - step) for step in y_steps]

    def f_x_first(i):
        send(fg.at[x, u_from[i], c], fg.at[x, u_from[i], c], fx_s.at[i, 0], fx_r.at[i, 0], at_x(xa))
        send(fg.at[x, u_from[i], c], fg.at[x, u_from[i], c], fx_s.at[i, 1], fx_r.at[i, 1], at_x(xb))

    def f_x_second(i):
        arrived(fg.at[xb, u_from[i], c], fx_r.at[i, 0])
        send(fg.at[xb, u_from[i], c], fg.at[xb, u_from[i], c], fx_s.at[i, 2], fx_r.at[i, 2], at_x(xa))

    f_x_first(0)
    target = leaf
    for t in range(2):
        for core in range(2):
            rows = r_ref.at[pl.ds(core * 64, 64)]
            place = rg.at[x, u, core]
            mine = jnp.logical_and(jnp.logical_and(h == t, c == core), u == target)

            @pl.when(mine)
            def _():
                pltpu.make_async_copy(rows, place, ry_r.at[u]).start()

            @pl.when(jnp.logical_not(mine))
            def _():
                pltpu.make_async_remote_copy(
                    src_ref=rows, dst_ref=place, send_sem=ry_s.at[t * 2 + core], recv_sem=ry_r.at[u],
                    device_id=(2 * t + core, x, target * NZ + z), device_id_type=MESH,
                ).start()
    for i, step in enumerate(y_steps):
        yy = lax.rem(y + step + 16, 8)
        send(l_ref.at[lax.div(yy, NU), quarter], lg.at[x, u, c], ly_s.at[i], ly_r.at[i], at_y(yy, c))

    za, zb = zmod(z + sgn), zmod(z - sgn)
    for d in range(1, NU):
        arrived(vall.at[z, umod(u - d)], vsc_r.at[d])

    def ring_z(array, part, ssem, rsem, forward, s):
        origin = zmod(z - sgn * (s - 1)) if forward else zmod(z + sgn * (s - 1))
        block = array.at[origin] if part is None else array.at[origin, part]
        if s > 1:
            arrived(block, rsem.at[s - 1])
        send(block, block, ssem.at[s], rsem.at[s], at_z(za if forward else zb))

    def ring_z_last(array, part, rsem, forward, s):
        origin = zmod(z - sgn * s) if forward else zmod(z + sgn * s)
        arrived(array.at[origin] if part is None else array.at[origin, part], rsem.at[s])

    low, high = pl.ds(0, 2), pl.ds(2, 2)
    rings = [(high, 0, True, 4), (high, 1, False, 3), (low, 2, True, 3), (low, 3, False, 4)]

    def v_step(s):
        for part, number, forward, last in rings:
            if s <= last:
                ring_z(vall, part, vz_s.at[number], vz_r.at[number], forward, s)

    v_step(1)
    for i in range(1, 4):
        arrived(fg.at[x, u_from[i], c], fy_r.at[i - 1])
        f_x_first(i)

    sibling = (h * 2 + 1 - c, x, col)

    def to_sibling(array, xx, i, ssem, rsem):
        send(array.at[xx, :, c], array.at[xx, :, c], ssem.at[i], rsem.at[i], sibling)

    x_from = [x, xb, xa, xmod(x - 2 * sgn)]
    to_sibling(fg, x, 0, fd_s, fd_r)
    v_step(2)
    f_x_second(0)
    f_x_second(1)
    v_step(3)
    f_x_second(2)
    f_x_second(3)
    to_sibling(fg, xb, 1, fd_s, fd_r)
    v_step(4)
    for i in range(4):
        arrived(fg.at[xa, u_from[i], c], fx_r.at[i, 1])
    to_sibling(fg, xa, 2, fd_s, fd_r)
    for i in range(4):
        arrived(rg.at[x, i, c], ry_r.at[i])

    def bulk_x_first(array, ssem, rsem):
        send(array.at[x, :, c], array.at[x, :, c], ssem.at[0], rsem.at[0], at_x(xa))
        send(array.at[x, :, c], array.at[x, :, c], ssem.at[1], rsem.at[1], at_x(xb))

    def bulk_x_second(array, ssem, rsem):
        arrived(array.at[xb, :, c], rsem.at[0])
        send(array.at[xb, :, c], array.at[xb, :, c], ssem.at[2], rsem.at[2], at_x(xa))

    bulk_x_first(rg, rx_s, rx_r)
    for i in range(4):
        arrived(fg.at[xmod(x - 2 * sgn), u_from[i], c], fx_r.at[i, 2])
    to_sibling(fg, x_from[3], 3, fd_s, fd_r)
    for i in range(1, 4):
        arrived(lg.at[x, u_from[i], c], ly_r.at[i - 1])
    bulk_x_first(lg, lx_s, lx_r)
    to_sibling(rg, x, 0, rd_s, rd_r)
    to_sibling(lg, x, 0, ld_s, ld_r)

    ring_z_last(vall, high, vz_r.at[0], True, 4)
    ring_z_last(vall, high, vz_r.at[1], False, 3)
    for i in range(4):
        xx = [x, xa, xb, xmod(x + 2 * sgn)][i]
        arrived(fg.at[xx, :, 1 - c], fd_r.at[i])

    def p_chunk(xx):
        return jnp.concatenate([vall[4 * (xx % 2) + i, 2 + xx // 2] for i in range(4)], axis=1)

    for pair in range(2):
        total = jnp.zeros((SUB, 256), F32)
        for xx in range(NX):
            total += dot_nt(p_chunk(xx), fg[xx, 2 * pair:2 * pair + 2].reshape(256, 512))
        acc[pair] = total
    ring_z_last(vall, low, vz_r.at[2], True, 3)
    ring_z_last(vall, low, vz_r.at[3], False, 4)
    for b in range(NU):
        block = b * NZ + z
        slot = jnp.int32(0)
        present = jnp.int32(0)
        for k in range(SLOTS):
            hit = map_ref[leaf, k] == block
            slot = jnp.where(hit, k, slot)
            present = jnp.where(hit, 1, present)
        padded = vall[lax.rem(slot, NZ), lax.div(slot, NZ)].astype(F32) * present.astype(F32)
        wm[u, b] = (padded - acc[b // 2, :, (b % 2) * BLK:(b % 2 + 1) * BLK]).astype(BF16)
    wk[z, u] = wm[u, u]

    for d in range(1, NU):
        to = umod(u + d)
        send(wm.at[u, to], wk.at[z, u], wc_s.at[d], wc_r.at[d], at_u(to))
    for d in range(1, NU):
        arrived(wk.at[z, umod(u - d)], wc_r.at[d])

    def w_step(s):
        ring_z(wk, None, wz_s.at[0], wz_r.at[0], True, s)
        if s <= 3:
            ring_z(wk, None, wz_s.at[1], wz_r.at[1], False, s)

    w_step(1)
    for d in range(1, NU):
        to = umod(u + d)
        send(wm.at[u], wm.at[u], wf_s.at[d], wf_r.at[d], at_u(to))
    bulk_x_second(rg, rx_s, rx_r)
    bulk_x_second(lg, lx_s, lx_r)
    w_step(2)
    for array, ssem, rsem, xsem in ((rg, rd_s, rd_r, rx_r), (lg, ld_s, ld_r, lx_r)):
        to_sibling(array, xb, 1, ssem, rsem)
        arrived(array.at[xa, :, c], xsem.at[1])
        to_sibling(array, xa, 2, ssem, rsem)
    w_step(3)
    for array, ssem, rsem, xsem in ((rg, rd_s, rd_r, rx_r), (lg, ld_s, ld_r, lx_r)):
        arrived(array.at[x_from[3], :, c], xsem.at[2])
        to_sibling(array, x_from[3], 3, ssem, rsem)
    w_step(4)
    for i in range(4):
        xx = [x, xa, xb, xmod(x + 2 * sgn)][i]
        arrived(lg.at[xx, :, 1 - c], ld_r.at[i])

    total = jnp.zeros((SUB, 256), F32)
    for xx in range(NX):
        total += dot_nt(p_chunk(xx), lg[xx].reshape(256, 512))
    lane = lax.broadcasted_iota(jnp.int32, (SUB, BLK), 1)
    odd = lax.rem(z, 2).astype(F32)
    l_sum = jnp.zeros((SUB, BLK), F32)
    for pair in range(2):
        first, second = (vall[4 * i + lax.div(z, 2), 2 + pair].astype(F32) for i in range(2))
        first_turned, second_turned = pltpu.roll(first, 64, 1), pltpu.roll(second, 64, 1)
        rows = jnp.where(
            lane < 64,
            first_turned * odd + first * (1.0 - odd),
            second * odd + second_turned * (1.0 - odd),
        )
        l_sum += rows * total[:, pair * BLK:(pair + 1) * BLK]

    for i in range(4):
        xx = [x, xa, xb, xmod(x + 2 * sgn)][i]
        arrived(rg.at[xx, :, 1 - c], rd_r.at[i])
    for d in range(1, NU):
        arrived(wm.at[umod(u - d)], wf_r.at[d])
    ring_z_last(wk, None, wz_r.at[1], False, 3)
    ring_z_last(wk, None, wz_r.at[0], True, 4)

    left = jnp.concatenate([wk[i].reshape(NU * SUB, BLK) for i in range(NZ)], axis=1)
    part = jnp.zeros((NU * SUB, BLK), F32)
    for pair in range(2):
        right = jnp.concatenate([rg[xx, 2 * pair:2 * pair + 2].reshape(256, 256) for xx in range(NX)], axis=1)
        term = dot_nt(left, right)
        for i in range(2):
            rows = wm[:, 2 * pair + i].reshape(NU * SUB, BLK).astype(F32)
            part += rows * term[:, i * BLK:(i + 1) * BLK]
    sums[...] = part
    own_rows = pl.ds(pl.multiple_of(u * SUB, SUB), SUB)
    sums[own_rows, :] = sums[own_rows, :] + l_sum
    flat = jnp.sum(jnp.transpose(sums[...]), axis=0, keepdims=True)
    red1[z] = jnp.concatenate(
        [flat[:, i * BLK:(i + 1) * BLK] for i in range(3)] + [jnp.zeros((5, BLK), F32)], axis=0
    )
    for d in range(1, NZ):
        send(red1.at[z], red1.at[z], d1_s.at[d], d1_r.at[d], at_z(zmod(z + d)))
    for d in range(1, NZ):
        arrived(red1.at[zmod(z - d)], d1_r.at[d])
    red2[u] = jnp.sum(red1[...], axis=0)
    for d in range(1, NU):
        send(red2.at[u], red2.at[u], d2_s.at[d], d2_r.at[d], at_u(umod(u + d)))
    for d in range(1, NU):
        arrived(red2.at[umod(u - d)], d2_r.at[d])
    result = jnp.sum(red2[...], axis=0)
    out_ref[...] = loc_ref[...] + jnp.concatenate([result[i:i + 1] for i in range(3)], axis=1)

    for copy in started:
        copy.wait_send()
    for t in range(2):
        for core in range(2):
            mine = jnp.logical_and(jnp.logical_and(h == t, c == core), u == target)

            @pl.when(jnp.logical_not(mine))
            def _():
                pltpu.make_async_remote_copy(
                    src_ref=r_ref.at[pl.ds(core * 64, 64)], dst_ref=rg.at[x, u, core],
                    send_sem=ry_s.at[t * 2 + core], recv_sem=ry_r.at[u],
                    device_id=(2 * t + core, x, target * NZ + z), device_id_type=MESH,
                ).wait_send()


def local(root_inverse, factor_first, local_first, factor_second, local_second, ancestor_map):
    vmem = pl.BlockSpec(memory_space=pltpu.VMEM)
    dma = pltpu.SemaphoreType.DMA
    scratch = [
        pltpu.VMEM((NU, SUB, BLK), BF16),
        pltpu.VMEM((NZ, NU, SUB, BLK), BF16),
        pltpu.VMEM((NX, NU, 2, 64, 512), BF16),
        pltpu.VMEM((NX, NU, 2, 32, 512), BF16),
        pltpu.VMEM((NX, NU, 2, 64, 256), BF16),
        pltpu.VMEM((NZ, NU, SUB, BLK), BF16),
        pltpu.VMEM((NU, NU, SUB, BLK), BF16),
        pltpu.VMEM((2, SUB, 256), F32),
        pltpu.VMEM((NU * SUB, BLK), F32),
        pltpu.VMEM((NZ, 8, BLK), F32),
        pltpu.VMEM((NU, 8, BLK), F32),
        dma((2,)),
    ]
    for count in ((4,), (4, 5), (3,), (4, 3), (4,), (3,), (3,), (4,), (4,), (3,), (4,), (4,), (4,), (2, 5), (8,), (4,)):
        scratch += [dma(count), dma(count)]
    return pl.pallas_call(
        kernel,
        out_shape=jax.ShapeDtypeStruct(local_second.shape, F32),
        in_specs=[vmem, vmem, vmem, vmem, vmem, pl.BlockSpec(memory_space=pltpu.SMEM)],
        out_specs=vmem,
        scratch_shapes=scratch,
        compiler_params=pltpu.CompilerParams(
            collective_id=0, has_side_effects=True, vmem_limit_bytes=32 * 1024 * 1024
        ),
        name="variances",
    )(root_inverse, factor_first, local_first, factor_second, local_second, ancestor_map)


def solution(mesh):
    placed = (
        P("col", ("leaf", "row")),
        P(None, "col", "row"),
        P(None, "col", "row"),
        P("leaf", "col", "row"),
        P("leaf", "row"),
        P(),
    )
    return jax.shard_map(
        local, mesh=mesh, in_specs=placed, out_specs=P("leaf", "row"), check_vma=False
    )
```

```python
import jax
import jax.numpy as jnp
from jax import lax
from jax.experimental import pallas as pl
from jax.experimental.pallas import tpu as pltpu
from jax.sharding import PartitionSpec as P

NX, NU, NZ = 4, 4, 8
BLK = 128
SUB = 96
SLOTS = 16
MESH = pl.DeviceIdType.MESH
BF16, F32 = jnp.bfloat16, jnp.float32
NT = (((1,), (1,)), ((), ()))


def dot_nt(a, b):
    return lax.dot_general(a, b, NT, preferred_element_type=F32)


def kernel(
    r_hbm, f_hbm, l_hbm, v_hbm, loc_hbm, map_hbm, out_ref,
    r_in, f_in, l_in, v_in, loc_in, map_in,
    vs, vall, fg, lg, rg, wk, wm, acc, zacc, sums, l_acc, red,
    in_sem, vsc_s, vsc_r, vz_s, vz_r, fy_s, fy_r, fx_s, fx_r, fd_s, fd_r,
    ly_s, ly_r, lx_s, lx_r, ld_s, ld_r, ry_s, ry_r, rx_s, rx_r, rd_s, rd_r,
    wc_s, wc_r, wf_s, wf_r, wz_s, wz_r, red_s, red_r,
):
    leaf, x, col = lax.axis_index("leaf"), lax.axis_index("row"), lax.axis_index("col")
    h, c = lax.div(leaf, 2), lax.rem(leaf, 2)
    u, z = lax.div(col, NZ), lax.rem(col, NZ)
    y = h * NU + u
    sgn = 1 - 2 * c

    def at_z(zz):
        return (leaf, x, u * NZ + zz)

    def at_u(uu):
        return (leaf, x, uu * NZ + z)

    def at_x(xx):
        return (leaf, xx, col)

    def at_y(yy, core):
        return (lax.div(yy, NU) * 2 + core, x, lax.rem(yy, NU) * NZ + z)

    def zmod(v):
        return lax.rem(v + 2 * NZ, NZ)

    def xmod(v):
        return lax.rem(v + 2 * NX, NX)

    def umod(v):
        return lax.rem(v + 2 * NU, NU)

    started = []

    def send(src, dst, ssem, rsem, to):
        copy = pltpu.make_async_remote_copy(
            src_ref=src, dst_ref=dst, send_sem=ssem, recv_sem=rsem, device_id=to, device_id_type=MESH
        )
        copy.start()
        started.append(copy)

    def settle():
        while started:
            started.pop(0).wait_send()

    def arrived(dst, rsem):
        pltpu.make_async_remote_copy(
            src_ref=dst, dst_ref=dst, send_sem=rsem, recv_sem=rsem, device_id=at_z(zmod(z + 1)), device_id_type=MESH
        ).wait_recv()

    barrier = pltpu.get_barrier_semaphore()
    peers = []
    for d in range(1, 16):
        number = lax.rem(y * 2 + c + d, 16)
        peers.append(at_y(lax.div(number, 2), lax.rem(number, 2)))
    peers += [at_z(zmod(z + d)) for d in (1, 2, 6, 7)]
    peers += [at_x(xmod(x + 1)), at_x(xmod(x - 1))]
    v_copy = pltpu.make_async_copy(v_hbm.at[0], v_in, in_sem.at[0])
    v_copy.start()
    for peer in peers:
        pl.semaphore_signal(barrier, inc=1, device_id=peer, device_id_type=MESH)

    half = pl.ds(pl.multiple_of(c * 64, 64), 64)
    quarter = pl.ds(pl.multiple_of(c * 32, 32), 32)
    loads = [
        pltpu.make_async_copy(f_hbm.at[:, half], f_in, in_sem.at[1]),
        pltpu.make_async_copy(f_hbm.at[h, half], fg.at[x, u, c], in_sem.at[2]),
        pltpu.make_async_copy(r_hbm, r_in, in_sem.at[3]),
        pltpu.make_async_copy(l_hbm.at[:, quarter], l_in, in_sem.at[4]),
        pltpu.make_async_copy(l_hbm.at[h, quarter], lg.at[x, u, c], in_sem.at[5]),
        pltpu.make_async_copy(loc_hbm, loc_in, in_sem.at[6]),
        pltpu.make_async_copy(map_hbm, map_in, in_sem.at[7]),
    ]
    for copy in loads:
        copy.start()
    v_copy.wait()
    vs[...] = jnp.transpose(v_in[...].astype(F32)).astype(BF16).reshape(NU, SUB, BLK)
    for copy in loads:
        copy.wait()
    pl.semaphore_wait(barrier, len(peers))

    pltpu.make_async_copy(vs.at[u], vall.at[z, u], vsc_r.at[u]).start()
    for d in range(1, NU):
        to = umod(u + d)
        send(vs.at[to], vall.at[z, u], vsc_s.at[d], vsc_r.at[u], at_u(to))
    xa, xb, xo = xmod(x + sgn), xmod(x - sgn), xmod(x + 2)
    y_steps = [sgn, -sgn, 2 * sgn]
    for i, step in enumerate(y_steps):
        yy = lax.rem(y + step + 16, 8)
        send(f_in.at[lax.div(yy, NU)], fg.at[x, u, c], fy_s.at[i], fy_r.at[i], at_y(yy, c))
    u_from = [u] + [umod(u - step) for step in y_steps]

    def f_x_first(i):
        if i > 0:
            arrived(fg.at[x, u_from[i], c], fy_r.at[i - 1])
        send(fg.at[x, u_from[i], c], fg.at[x, u_from[i], c], fx_s.at[i, 0], fx_r.at[i, 0], at_x(xa))
        send(fg.at[x, u_from[i], c], fg.at[x, u_from[i], c], fx_s.at[i, 1], fx_r.at[i, 1], at_x(xb))

    def f_x_second(i):
        arrived(fg.at[xb, u_from[i], c], fx_r.at[i, 0])
        send(fg.at[xb, u_from[i], c], fg.at[xb, u_from[i], c], fx_s.at[i, 2], fx_r.at[i, 2], at_x(xa))

    def z_first(array, part, ssem, rsem, way):
        block = array.at[z, part]
        send(block, block, ssem.at[2], rsem.at[2], at_z(zmod(z + 2 * way)))
        send(block, block, ssem.at[1], rsem.at[1], at_z(zmod(z + way)))

    def z_second(array, part, ssem, rsem, way, last):
        block = array.at[zmod(z - 2 * way), part]
        arrived(block, rsem.at[2])
        if last == 4:
            send(block, block, ssem.at[4], rsem.at[4], at_z(zmod(z + 2 * way)))
        send(block, block, ssem.at[3], rsem.at[3], at_z(zmod(z + way)))

    def z_last(array, part, rsem, way, numbers):
        for number in numbers:
            arrived(array.at[zmod(z - number * way), part], rsem.at[number])

    upper, lower = pl.ds(2, 2), pl.ds(0, 2)

    def v_first(part, number):
        z_first(vall, part, vz_s.at[number], vz_r.at[number], sgn)
        z_first(vall, part, vz_s.at[number + 1], vz_r.at[number + 1], -sgn)

    def v_second(part, number):
        z_second(vall, part, vz_s.at[number], vz_r.at[number], sgn, 4)
        z_second(vall, part, vz_s.at[number + 1], vz_r.at[number + 1], -sgn, 3)

    def v_last(part, number):
        z_last(vall, part, vz_r.at[number], sgn, (1, 3, 4))
        z_last(vall, part, vz_r.at[number + 1], -sgn, (1, 3))

    sibling = (h * 2 + 1 - c, x, col)

    def to_sibling(array, xx, i, ssem, rsem):
        send(array.at[xx, :, c], array.at[xx, :, c], ssem.at[i], rsem.at[i], sibling)

    def from_sibling(array, rsem, places):
        for i, xx in enumerate(places):
            arrived(array.at[xx, :, 1 - c], rsem.at[i])

    def bulk_x_first(array, ssem, rsem):
        send(array.at[x, :, c], array.at[x, :, c], ssem.at[0], rsem.at[0], at_x(xa))
        send(array.at[x, :, c], array.at[x, :, c], ssem.at[1], rsem.at[1], at_x(xb))

    def bulk_x_second(array, ssem, rsem):
        arrived(array.at[xb, :, c], rsem.at[0])
        send(array.at[xb, :, c], array.at[xb, :, c], ssem.at[2], rsem.at[2], at_x(xa))

    f_x_first(0)
    arrived(vall.at[z, 2], vsc_r.at[2])
    arrived(vall.at[z, 3], vsc_r.at[3])
    v_first(upper, 0)
    f_x_first(1)
    f_x_first(2)
    arrived(vall.at[z, 0], vsc_r.at[0])
    arrived(vall.at[z, 1], vsc_r.at[1])
    v_first(lower, 2)
    f_x_second(0)
    f_x_first(3)
    to_sibling(fg, x, 0, fd_s, fd_r)
    target = leaf
    r_sends = []
    for t in range(2):
        for core in range(2):
            rows = r_in.at[pl.ds(core * 64, 64)]
            place = rg.at[x, u, core]
            mine = jnp.logical_and(jnp.logical_and(h == t, c == core), u == target)
            copy = pltpu.make_async_remote_copy(
                src_ref=rows, dst_ref=place, send_sem=ry_s.at[t * 2 + core], recv_sem=ry_r.at[u],
                device_id=(2 * t + core, x, target * NZ + z), device_id_type=MESH,
            )
            r_sends.append((mine, copy))

            @pl.when(mine)
            def _():
                pltpu.make_async_copy(rows, place, ry_r.at[u]).start()

            @pl.when(jnp.logical_not(mine))
            def _():
                copy.start()
    v_second(upper, 0)
    f_x_second(1)
    f_x_second(2)
    v_second(lower, 2)
    for i, step in enumerate(y_steps):
        yy = lax.rem(y + step + 16, 8)
        send(l_in.at[lax.div(yy, NU)], lg.at[x, u, c], ly_s.at[i], ly_r.at[i], at_y(yy, c))
    f_x_second(3)
    to_sibling(fg, xb, 1, fd_s, fd_r)
    for i in range(4):
        arrived(fg.at[xa, u_from[i], c], fx_r.at[i, 1])
    to_sibling(fg, xa, 2, fd_s, fd_r)
    for i in range(4):
        block = fg.at[xo, u_from[i], c]
        arrived(block, fx_r.at[i, 2])
        send(block, block, fd_s.at[3 + i], fd_r.at[3 + i], sibling)
    for i in range(4):
        arrived(rg.at[x, i, c], ry_r.at[i])
    bulk_x_first(rg, rx_s, rx_r)
    for i in range(1, 4):
        arrived(lg.at[x, u_from[i], c], ly_r.at[i - 1])
    bulk_x_first(lg, lx_s, lx_r)
    v_last(upper, 0)
    from_sibling(fg, fd_r, (x, xa, xb))
    for i, uu in enumerate([u] + [umod(u + step) for step in y_steps]):
        arrived(fg.at[xo, uu, 1 - c], fd_r.at[3 + i])

    def p_chunk(xx):
        return jnp.concatenate([vall[4 * (xx % 2) + i, 2 + xx // 2] for i in range(4)], axis=1)

    for pair in range(2):
        total = jnp.zeros((SUB, 256), F32)
        for xx in range(NX):
            total += dot_nt(p_chunk(xx), fg[xx, 2 * pair:2 * pair + 2].reshape(256, 512))
        acc[pair] = total
    v_last(lower, 2)
    for b in range(NU):
        block = b * NZ + z
        slot = jnp.int32(0)
        present = jnp.int32(0)
        for k in range(SLOTS):
            hit = map_in[leaf, k] == block
            slot = jnp.where(hit, k, slot)
            present = jnp.where(hit, 1, present)
        padded = vall[lax.rem(slot, NZ), lax.div(slot, NZ)].astype(F32) * present.astype(F32)
        wm[u, b] = (padded - acc[b // 2, :, (b % 2) * BLK:(b % 2 + 1) * BLK]).astype(BF16)

    pltpu.make_async_copy(wm.at[u, u], wk.at[z, u], wc_r.at[0]).start()
    for d in range(1, NU):
        to = umod(u + d)
        send(wm.at[u, to], wk.at[z, u], wc_s.at[d], wc_r.at[d], at_u(to))
    order = (0, 1, 3, 2)
    parts = [pl.ds(umod(u - d), 1) for d in order]
    for k in range(NU):
        arrived(wk.at[z, parts[k]], wc_r.at[order[k]])
        z_first(wk, parts[k], wz_s.at[k], wz_r.at[k], -sgn)
        if k == 0:
            for d in range(1, NU):
                to = umod(u + d)
                send(wm.at[u], wm.at[u], wf_s.at[d], wf_r.at[d], at_u(to))
    for array, xs, xr, ds, dr in ((rg, rx_s, rx_r, rd_s, rd_r), (lg, lx_s, lx_r, ld_s, ld_r)):
        bulk_x_second(array, xs, xr)
        to_sibling(array, x, 0, ds, dr)
        to_sibling(array, xb, 1, ds, dr)
        arrived(array.at[xa, :, c], xr.at[1])
        to_sibling(array, xa, 2, ds, dr)
    for k in range(NU):
        z_second(wk, parts[k], wz_s.at[k], wz_r.at[k], -sgn, 4)
    for array, xr, ds, dr in ((rg, rx_r, rd_s, rd_r), (lg, lx_r, ld_s, ld_r)):
        arrived(array.at[xo, :, c], xr.at[2])
        to_sibling(array, xo, 3, ds, dr)

    from_sibling(lg, ld_r, (x, xa, xb, xo))
    total = jnp.zeros((SUB, 256), F32)
    for xx in range(NX):
        total += dot_nt(p_chunk(xx), lg[xx].reshape(256, 512))
    lane = lax.broadcasted_iota(jnp.int32, (SUB, BLK), 1)
    odd = lax.rem(z, 2).astype(F32)
    l_sum = jnp.zeros((SUB, BLK), F32)
    for pair in range(2):
        one, two = (vall[4 * i + lax.div(z, 2), 2 + pair].astype(F32) for i in range(2))
        one_turned, two_turned = pltpu.roll(one, 64, 1), pltpu.roll(two, 64, 1)
        rows = jnp.where(
            lane < 64, one_turned * odd + one * (1.0 - odd), two * odd + two_turned * (1.0 - odd)
        )
        l_sum += rows * total[:, pair * BLK:(pair + 1) * BLK]
    l_acc[...] = l_sum
    from_sibling(rg, rd_r, (x, xa, xb, xo))
    settle()

    def w_rows(d):
        block = wk[zmod(z + sgn * d)].reshape(NU * SUB, BLK)
        return block * 2 if 1 <= d <= 3 else block

    def r_block(pair, d):
        zz = zmod(z + sgn * d)
        lanes = pl.ds(pl.multiple_of(lax.rem(zz, 2) * BLK, BLK), BLK)
        return rg[lax.div(zz, 2), 2 * pair:2 * pair + 2, :, :, lanes].reshape(256, BLK)

    for k in range(NU):
        z_last(wk, parts[k], wz_r.at[k], -sgn, (1, 3))
    left = jnp.concatenate([w_rows(d) for d in range(4)], axis=1)
    for pair in range(2):
        zacc[pair] = dot_nt(left, jnp.concatenate([r_block(pair, d) for d in range(4)], axis=1))
    for d in range(1, NU):
        arrived(wm.at[umod(u - d)], wf_r.at[d])
    for k in range(NU):
        z_last(wk, parts[k], wz_r.at[k], -sgn, (4,))
    part = jnp.zeros((NU * SUB, BLK), F32)
    for pair in range(2):
        term = zacc[pair] + dot_nt(w_rows(4), r_block(pair, 4))
        for i in range(2):
            rows = wm[:, 2 * pair + i].reshape(NU * SUB, BLK).astype(F32)
            part += rows * term[:, i * BLK:(i + 1) * BLK]
    sums[...] = part
    own_rows = pl.ds(pl.multiple_of(u * SUB, SUB), SUB)
    sums[own_rows, :] = sums[own_rows, :] + l_acc[...]
    flat = jnp.sum(jnp.transpose(sums[...]), axis=0, keepdims=True)
    red[z, u] = jnp.concatenate(
        [flat[:, i * BLK:(i + 1) * BLK] for i in range(3)] + [jnp.zeros((5, BLK), F32)], axis=0
    )
    pairs = [(dz, du) for du in (2, 3, 1, 0) for dz in (4, 3, 5, 2, 6, 1, 7, 0) if dz or du]
    for i, (dz, du) in enumerate(pairs):
        to = (leaf, x, umod(u + du) * NZ + zmod(z + dz))
        send(red.at[z, u], red.at[z, u], red_s.at[i], red_r.at[i], to)
    for i, (dz, du) in enumerate(pairs):
        arrived(red.at[zmod(z - dz), umod(u - du)], red_r.at[i])
    result = jnp.sum(red[...].reshape(NZ * NU, 8, BLK), axis=0)
    out_ref[...] = loc_in[...] + jnp.concatenate([result[i:i + 1] for i in range(3)], axis=1)

    settle()
    for mine, copy in r_sends:
        @pl.when(jnp.logical_not(mine))
        def _():
            copy.wait_send()


def local(root_inverse, factor_first, local_first, factor_second, local_second, ancestor_map):
    dma = pltpu.SemaphoreType.DMA
    scratch = [
        pltpu.VMEM(root_inverse.shape, BF16),
        pltpu.VMEM((2, 64, 512), BF16),
        pltpu.VMEM((2, 32, 512), BF16),
        pltpu.VMEM(factor_second.shape[1:], BF16),
        pltpu.VMEM(local_second.shape, F32),
        pltpu.SMEM(ancestor_map.shape, jnp.int32),
        pltpu.VMEM((NU, SUB, BLK), BF16),
        pltpu.VMEM((NZ, NU, SUB, BLK), BF16),
        pltpu.VMEM((NX, NU, 2, 64, 512), BF16),
        pltpu.VMEM((NX, NU, 2, 32, 512), BF16),
        pltpu.VMEM((NX, NU, 2, 64, 256), BF16),
        pltpu.VMEM((NZ, NU, SUB, BLK), BF16),
        pltpu.VMEM((NU, NU, SUB, BLK), BF16),
        pltpu.VMEM((2, SUB, 256), F32),
        pltpu.VMEM((2, NU * SUB, 256), F32),
        pltpu.VMEM((NU * SUB, BLK), F32),
        pltpu.VMEM((SUB, BLK), F32),
        pltpu.VMEM((NZ, NU, 8, BLK), F32),
        dma((8,)),
    ]
    for count in ((4,), (4, 5), (3,), (4, 3), (7,), (3,), (3,), (4,), (4,), (3,), (4,), (4,), (4,), (4, 5), (31,)):
        scratch += [dma(count), dma(count)]
    return pl.pallas_call(
        kernel,
        out_shape=jax.ShapeDtypeStruct(local_second.shape, F32),
        in_specs=[pl.BlockSpec(memory_space=pltpu.HBM)] * 6,
        out_specs=pl.BlockSpec(memory_space=pltpu.VMEM),
        scratch_shapes=scratch,
        compiler_params=pltpu.CompilerParams(
            collective_id=0, has_side_effects=True, vmem_limit_bytes=65_000_000
        ),
        name="variances",
    )(root_inverse, factor_first, local_first, factor_second, local_second, ancestor_map)


def solution(mesh):
    placed = (
        P("col", ("leaf", "row")),
        P(None, "col", "row"),
        P(None, "col", "row"),
        P("leaf", "col", "row"),
        P("leaf", "row"),
        P(),
    )
    return jax.shard_map(
        local, mesh=mesh, in_specs=placed, out_specs=P("leaf", "row"), check_vma=False
    )
```

```python
import jax
import jax.numpy as jnp
from jax import lax
from jax.experimental import pallas as pl
from jax.experimental.pallas import tpu as pltpu
from jax.sharding import PartitionSpec as P

NX, NU, NZ = 4, 4, 8
BLK = 128
SUB = 96
SLOTS = 16
MESH = pl.DeviceIdType.MESH
BF16, F32 = jnp.bfloat16, jnp.float32
NT = (((1,), (1,)), ((), ()))


def dot_nt(a, b):
    return lax.dot_general(a, b, NT, preferred_element_type=F32)


def kernel(
    r_hbm, f_hbm, l_hbm, v_hbm, loc_hbm, map_hbm, out_ref,
    r_in, f_in, l_in, v_in, loc_in, map_in,
    vs, vall, fg, lg, rg, wk, wm, acc, zacc, sums, l_acc, red,
    in_sem, vsc_s, vsc_r, vz_s, vz_r, fy_s, fy_r, fx_s, fx_r, fd_s, fd_r,
    ly_s, ly_r, lx_s, lx_r, ld_s, ld_r, ry_s, ry_r, rx_s, rx_r, rd_s, rd_r,
    wc_s, wc_r, wf_s, wf_r, wz_s, wz_r, red_s, red_r,
):
    leaf, x, col = lax.axis_index("leaf"), lax.axis_index("row"), lax.axis_index("col")
    h, c = lax.div(leaf, 2), lax.rem(leaf, 2)
    u, z = lax.div(col, NZ), lax.rem(col, NZ)
    y = h * NU + u
    sgn = 1 - 2 * c

    def at_z(zz):
        return (leaf, x, u * NZ + zz)

    def at_u(uu):
        return (leaf, x, uu * NZ + z)

    def at_x(xx):
        return (leaf, xx, col)

    def at_y(yy, core):
        return (lax.div(yy, NU) * 2 + core, x, lax.rem(yy, NU) * NZ + z)

    def zmod(v):
        return lax.rem(v + 2 * NZ, NZ)

    def xmod(v):
        return lax.rem(v + 2 * NX, NX)

    def umod(v):
        return lax.rem(v + 2 * NU, NU)

    started = []

    def send(src, dst, ssem, rsem, to):
        copy = pltpu.make_async_remote_copy(
            src_ref=src, dst_ref=dst, send_sem=ssem, recv_sem=rsem, device_id=to, device_id_type=MESH
        )
        copy.start()
        started.append(copy)

    def settle():
        while started:
            started.pop(0).wait_send()

    def arrived(dst, rsem):
        pltpu.make_async_remote_copy(
            src_ref=dst, dst_ref=dst, send_sem=rsem, recv_sem=rsem, device_id=at_z(zmod(z + 1)), device_id_type=MESH
        ).wait_recv()

    barrier = pltpu.get_barrier_semaphore()
    peers = []
    for d in range(1, 16):
        number = lax.rem(y * 2 + c + d, 16)
        peers.append(at_y(lax.div(number, 2), lax.rem(number, 2)))
    peers += [at_z(zmod(z + d)) for d in (1, 2, 6, 7)]
    peers += [at_x(xmod(x + 1)), at_x(xmod(x - 1))]
    v_copy = pltpu.make_async_copy(v_hbm.at[0], v_in, in_sem.at[0])
    v_copy.start()
    for peer in peers:
        pl.semaphore_signal(barrier, inc=1, device_id=peer, device_id_type=MESH)

    half = pl.ds(pl.multiple_of(c * 64, 64), 64)
    quarter = pl.ds(pl.multiple_of(c * 32, 32), 32)
    loads = [
        pltpu.make_async_copy(f_hbm.at[:, half], f_in, in_sem.at[1]),
        pltpu.make_async_copy(f_hbm.at[h, half], fg.at[x, u, c], in_sem.at[2]),
        pltpu.make_async_copy(r_hbm, r_in, in_sem.at[3]),
        pltpu.make_async_copy(l_hbm.at[:, quarter], l_in, in_sem.at[4]),
        pltpu.make_async_copy(l_hbm.at[h, quarter], lg.at[x, u, c], in_sem.at[5]),
        pltpu.make_async_copy(loc_hbm, loc_in, in_sem.at[6]),
        pltpu.make_async_copy(map_hbm, map_in, in_sem.at[7]),
    ]
    for copy in loads:
        copy.start()
    v_copy.wait()
    vs[...] = jnp.transpose(v_in[...].astype(F32)).astype(BF16).reshape(NU, SUB, BLK)
    for copy in loads:
        copy.wait()
    pl.semaphore_wait(barrier, len(peers))

    pltpu.make_async_copy(vs.at[u], vall.at[z, u], vsc_r.at[u]).start()
    for d in range(1, NU):
        to = umod(u + d)
        send(vs.at[to], vall.at[z, u], vsc_s.at[d], vsc_r.at[u], at_u(to))
    xa, xb, xo = xmod(x + sgn), xmod(x - sgn), xmod(x + 2)
    y_steps = [sgn, -sgn, 2 * sgn]
    for i, step in enumerate(y_steps):
        yy = lax.rem(y + step + 16, 8)
        send(f_in.at[lax.div(yy, NU)], fg.at[x, u, c], fy_s.at[i], fy_r.at[i], at_y(yy, c))
    u_from = [u] + [umod(u - step) for step in y_steps]

    def f_x_first(i):
        if i > 0:
            arrived(fg.at[x, u_from[i], c], fy_r.at[i - 1])
        send(fg.at[x, u_from[i], c], fg.at[x, u_from[i], c], fx_s.at[i, 0], fx_r.at[i, 0], at_x(xa))
        send(fg.at[x, u_from[i], c], fg.at[x, u_from[i], c], fx_s.at[i, 1], fx_r.at[i, 1], at_x(xb))

    def f_x_second(i):
        arrived(fg.at[xb, u_from[i], c], fx_r.at[i, 0])
        send(fg.at[xb, u_from[i], c], fg.at[xb, u_from[i], c], fx_s.at[i, 2], fx_r.at[i, 2], at_x(xa))

    def z_first(array, part, ssem, rsem, way):
        block = array.at[z, part]
        send(block, block, ssem.at[2], rsem.at[2], at_z(zmod(z + 2 * way)))
        send(block, block, ssem.at[1], rsem.at[1], at_z(zmod(z + way)))

    def z_second(array, part, ssem, rsem, way, last):
        block = array.at[zmod(z - 2 * way), part]
        arrived(block, rsem.at[2])
        if last == 4:
            send(block, block, ssem.at[4], rsem.at[4], at_z(zmod(z + 2 * way)))
        send(block, block, ssem.at[3], rsem.at[3], at_z(zmod(z + way)))

    def z_last(array, part, rsem, way, numbers):
        for number in numbers:
            arrived(array.at[zmod(z - number * way), part], rsem.at[number])

    upper, lower = pl.ds(2, 2), pl.ds(0, 2)

    def v_first(part, number):
        z_first(vall, part, vz_s.at[number], vz_r.at[number], sgn)
        z_first(vall, part, vz_s.at[number + 1], vz_r.at[number + 1], -sgn)

    def v_second(part, number):
        z_second(vall, part, vz_s.at[number], vz_r.at[number], sgn, 4)
        z_second(vall, part, vz_s.at[number + 1], vz_r.at[number + 1], -sgn, 3)

    def v_last(part, number):
        z_last(vall, part, vz_r.at[number], sgn, (1, 3, 4))
        z_last(vall, part, vz_r.at[number + 1], -sgn, (1, 3))

    sibling = (h * 2 + 1 - c, x, col)

    def to_sibling(array, xx, i, ssem, rsem):
        send(array.at[xx, :, c], array.at[xx, :, c], ssem.at[i], rsem.at[i], sibling)

    def from_sibling(array, rsem, places):
        for i, xx in enumerate(places):
            arrived(array.at[xx, :, 1 - c], rsem.at[i])

    def bulk_x_first(array, ssem, rsem):
        send(array.at[x, :, c], array.at[x, :, c], ssem.at[0], rsem.at[0], at_x(xa))
        send(array.at[x, :, c], array.at[x, :, c], ssem.at[1], rsem.at[1], at_x(xb))

    def bulk_x_second(array, ssem, rsem):
        arrived(array.at[xb, :, c], rsem.at[0])
        send(array.at[xb, :, c], array.at[xb, :, c], ssem.at[2], rsem.at[2], at_x(xa))

    f_x_first(0)
    arrived(vall.at[z, 2], vsc_r.at[2])
    arrived(vall.at[z, 3], vsc_r.at[3])
    v_first(upper, 0)
    f_x_first(1)
    f_x_first(2)
    arrived(vall.at[z, 0], vsc_r.at[0])
    arrived(vall.at[z, 1], vsc_r.at[1])
    v_first(lower, 2)
    f_x_second(0)
    f_x_first(3)
    to_sibling(fg, x, 0, fd_s, fd_r)
    target = leaf
    r_sends = []
    for t in range(2):
        for core in range(2):
            rows = r_in.at[pl.ds(core * 64, 64)]
            place = rg.at[x, u, core]
            mine = jnp.logical_and(jnp.logical_and(h == t, c == core), u == target)
            copy = pltpu.make_async_remote_copy(
                src_ref=rows, dst_ref=place, send_sem=ry_s.at[t * 2 + core], recv_sem=ry_r.at[u],
                device_id=(2 * t + core, x, target * NZ + z), device_id_type=MESH,
            )
            r_sends.append((mine, copy))

            @pl.when(mine)
            def _():
                pltpu.make_async_copy(rows, place, ry_r.at[u]).start()

            @pl.when(jnp.logical_not(mine))
            def _():
                copy.start()
    v_second(upper, 0)
    f_x_second(1)
    f_x_second(2)
    f_x_second(3)
    to_sibling(fg, xb, 1, fd_s, fd_r)
    v_second(lower, 2)
    for i, step in enumerate(y_steps):
        yy = lax.rem(y + step + 16, 8)
        send(l_in.at[lax.div(yy, NU)], lg.at[x, u, c], ly_s.at[i], ly_r.at[i], at_y(yy, c))
    for i in range(4):
        arrived(fg.at[xa, u_from[i], c], fx_r.at[i, 1])
    to_sibling(fg, xa, 2, fd_s, fd_r)
    for i in range(4):
        block = fg.at[xo, u_from[i], c]
        arrived(block, fx_r.at[i, 2])
        send(block, block, fd_s.at[3 + i], fd_r.at[3 + i], sibling)
    for i in range(4):
        arrived(rg.at[x, i, c], ry_r.at[i])
    bulk_x_first(rg, rx_s, rx_r)
    for i in range(1, 4):
        arrived(lg.at[x, u_from[i], c], ly_r.at[i - 1])
    bulk_x_first(lg, lx_s, lx_r)
    v_last(upper, 0)
    from_sibling(fg, fd_r, (x, xa, xb))
    for i, uu in enumerate([u] + [umod(u + step) for step in y_steps]):
        arrived(fg.at[xo, uu, 1 - c], fd_r.at[3 + i])

    def p_chunk(xx):
        return jnp.concatenate([vall[4 * (xx % 2) + i, 2 + xx // 2] for i in range(4)], axis=1)

    for pair in range(2):
        total = jnp.zeros((SUB, 256), F32)
        for xx in range(NX):
            total += dot_nt(p_chunk(xx), fg[xx, 2 * pair:2 * pair + 2].reshape(256, 512))
        acc[pair] = total
    v_last(lower, 2)
    for b in range(NU):
        block = b * NZ + z
        slot = jnp.int32(0)
        present = jnp.int32(0)
        for k in range(SLOTS):
            hit = map_in[leaf, k] == block
            slot = jnp.where(hit, k, slot)
            present = jnp.where(hit, 1, present)
        padded = vall[lax.rem(slot, NZ), lax.div(slot, NZ)].astype(F32) * present.astype(F32)
        wm[u, b] = (padded - acc[b // 2, :, (b % 2) * BLK:(b % 2 + 1) * BLK]).astype(BF16)

    pltpu.make_async_copy(wm.at[u, u], wk.at[z, u], wc_r.at[0]).start()
    for d in range(1, NU):
        to = umod(u + d)
        send(wm.at[u, to], wk.at[z, u], wc_s.at[d], wc_r.at[d], at_u(to))
    order = (0, 1, 3, 2)
    parts = [pl.ds(umod(u - d), 1) for d in order]
    for k in range(NU):
        arrived(wk.at[z, parts[k]], wc_r.at[order[k]])
        z_first(wk, parts[k], wz_s.at[k], wz_r.at[k], -sgn)
    for d in range(1, NU):
        to = umod(u + d)
        for i in range(1, NU):
            rows = wm.at[u, umod(to + i)]
            send(rows, rows, wf_s.at[d, i], wf_r.at[d, i], at_u(to))
    for d in range(1, NU):
        wm[umod(u - d), u] = wk[z, umod(u - d)]
    for array, xs, xr, ds, dr in ((rg, rx_s, rx_r, rd_s, rd_r), (lg, lx_s, lx_r, ld_s, ld_r)):
        bulk_x_second(array, xs, xr)
        to_sibling(array, x, 0, ds, dr)
        to_sibling(array, xb, 1, ds, dr)
        arrived(array.at[xa, :, c], xr.at[1])
        to_sibling(array, xa, 2, ds, dr)
    for k in range(NU):
        z_second(wk, parts[k], wz_s.at[k], wz_r.at[k], -sgn, 4)
    for array, xr, ds, dr in ((rg, rx_r, rd_s, rd_r), (lg, lx_r, ld_s, ld_r)):
        arrived(array.at[xo, :, c], xr.at[2])
        to_sibling(array, xo, 3, ds, dr)

    from_sibling(lg, ld_r, (x, xa, xb, xo))
    total = jnp.zeros((SUB, 256), F32)
    for xx in range(NX):
        total += dot_nt(p_chunk(xx), lg[xx].reshape(256, 512))
    lane = lax.broadcasted_iota(jnp.int32, (SUB, BLK), 1)
    odd = lax.rem(z, 2).astype(F32)
    l_sum = jnp.zeros((SUB, BLK), F32)
    for pair in range(2):
        one, two = (vall[4 * i + lax.div(z, 2), 2 + pair].astype(F32) for i in range(2))
        one_turned, two_turned = pltpu.roll(one, 64, 1), pltpu.roll(two, 64, 1)
        rows = jnp.where(
            lane < 64, one_turned * odd + one * (1.0 - odd), two * odd + two_turned * (1.0 - odd)
        )
        l_sum += rows * total[:, pair * BLK:(pair + 1) * BLK]
    l_acc[...] = l_sum
    from_sibling(rg, rd_r, (x, xa, xb, xo))
    settle()

    def w_rows(d):
        block = wk[zmod(z + sgn * d)].reshape(NU * SUB, BLK)
        return block * 2 if 1 <= d <= 3 else block

    def r_block(pair, d):
        zz = zmod(z + sgn * d)
        lanes = pl.ds(pl.multiple_of(lax.rem(zz, 2) * BLK, BLK), BLK)
        return rg[lax.div(zz, 2), 2 * pair:2 * pair + 2, :, :, lanes].reshape(256, BLK)

    for k in range(NU):
        z_last(wk, parts[k], wz_r.at[k], -sgn, (1, 3))
    left = jnp.concatenate([w_rows(d) for d in range(4)], axis=1)
    for pair in range(2):
        zacc[pair] = dot_nt(left, jnp.concatenate([r_block(pair, d) for d in range(4)], axis=1))
    for d in range(1, NU):
        for i in range(1, NU):
            arrived(wm.at[umod(u - d), umod(u + i)], wf_r.at[d, i])
    for k in range(NU):
        z_last(wk, parts[k], wz_r.at[k], -sgn, (4,))
    part = jnp.zeros((NU * SUB, BLK), F32)
    for pair in range(2):
        term = zacc[pair] + dot_nt(w_rows(4), r_block(pair, 4))
        for i in range(2):
            rows = wm[:, 2 * pair + i].reshape(NU * SUB, BLK).astype(F32)
            part += rows * term[:, i * BLK:(i + 1) * BLK]
    sums[...] = part
    own_rows = pl.ds(pl.multiple_of(u * SUB, SUB), SUB)
    sums[own_rows, :] = sums[own_rows, :] + l_acc[...]
    flat = jnp.sum(jnp.transpose(sums[...]), axis=0, keepdims=True)
    me = z * NU + u
    red[me] = jnp.concatenate(
        [flat[:, i * BLK:(i + 1) * BLK] for i in range(3)] + [jnp.zeros((5, BLK), F32)], axis=0
    )
    others = [i + (i >= me).astype(jnp.int32) for i in range(NZ * NU - 1)]
    for i, other in enumerate(others):
        to = (leaf, x, lax.rem(other, NU) * NZ + lax.div(other, NU))
        send(red.at[me], red.at[me], red_s.at[i], red_r.at[me], to)
    for other in others:
        arrived(red.at[other], red_r.at[other])
    result = jnp.sum(red[...], axis=0)
    out_ref[...] = loc_in[...] + jnp.concatenate([result[i:i + 1] for i in range(3)], axis=1)

    settle()
    for mine, copy in r_sends:
        @pl.when(jnp.logical_not(mine))
        def _():
            copy.wait_send()


def local(root_inverse, factor_first, local_first, factor_second, local_second, ancestor_map):
    dma = pltpu.SemaphoreType.DMA
    scratch = [
        pltpu.VMEM(root_inverse.shape, BF16),
        pltpu.VMEM((2, 64, 512), BF16),
        pltpu.VMEM((2, 32, 512), BF16),
        pltpu.VMEM(factor_second.shape[1:], BF16),
        pltpu.VMEM(local_second.shape, F32),
        pltpu.SMEM(ancestor_map.shape, jnp.int32),
        pltpu.VMEM((NU, SUB, BLK), BF16),
        pltpu.VMEM((NZ, NU, SUB, BLK), BF16),
        pltpu.VMEM((NX, NU, 2, 64, 512), BF16),
        pltpu.VMEM((NX, NU, 2, 32, 512), BF16),
        pltpu.VMEM((NX, NU, 2, 64, 256), BF16),
        pltpu.VMEM((NZ, NU, SUB, BLK), BF16),
        pltpu.VMEM((NU, NU, SUB, BLK), BF16),
        pltpu.VMEM((2, SUB, 256), F32),
        pltpu.VMEM((2, NU * SUB, 256), F32),
        pltpu.VMEM((NU * SUB, BLK), F32),
        pltpu.VMEM((SUB, BLK), F32),
        pltpu.VMEM((NZ * NU, 8, BLK), F32),
        dma((8,)),
    ]
    for count in ((4,), (4, 5), (3,), (4, 3), (7,), (3,), (3,), (4,), (4,), (3,), (4,), (4,), (4, 4), (4, 5), (32,)):
        scratch += [dma(count), dma(count)]
    return pl.pallas_call(
        kernel,
        out_shape=jax.ShapeDtypeStruct(local_second.shape, F32),
        in_specs=[pl.BlockSpec(memory_space=pltpu.HBM)] * 6,
        out_specs=pl.BlockSpec(memory_space=pltpu.VMEM),
        scratch_shapes=scratch,
        compiler_params=pltpu.CompilerParams(
            collective_id=0, has_side_effects=True, vmem_limit_bytes=65_000_000
        ),
        name="variances",
    )(root_inverse, factor_first, local_first, factor_second, local_second, ancestor_map)


def solution(mesh):
    placed = (
        P("col", ("leaf", "row")),
        P(None, "col", "row"),
        P(None, "col", "row"),
        P("leaf", "col", "row"),
        P("leaf", "row"),
        P(),
    )
    return jax.shard_map(
        local, mesh=mesh, in_specs=placed, out_specs=P("leaf", "row"), check_vma=False
    )
```

```python
import jax
import jax.numpy as jnp
from jax import lax
from jax.experimental import pallas as pl
from jax.experimental.pallas import tpu as pltpu
from jax.sharding import PartitionSpec as P

NX, NU, NZ = 4, 4, 8
BLK = 128
SUB = 96
SLOTS = 16
MESH = pl.DeviceIdType.MESH
BF16, F32 = jnp.bfloat16, jnp.float32
NT = (((1,), (1,)), ((), ()))


def dot_nt(a, b):
    return lax.dot_general(a, b, NT, preferred_element_type=F32)


def kernel(
    r_hbm, f_hbm, l_hbm, v_hbm, loc_hbm, map_hbm, out_ref,
    r_in, f_in, l_in, v_in, loc_in, map_in,
    vs, vall, fg, lg, rg, wk, wm, acc, zacc, sums, l_acc, red,
    in_sem, vsc_s, vsc_r, vz_s, vz_r, fy_s, fy_r, fx_s, fx_r, fd_s, fd_r,
    ly_s, ly_r, lx_s, lx_r, ld_s, ld_r, ry_s, ry_r, rx_s, rx_r, rd_s, rd_r,
    wc_s, wc_r, wf_s, wf_r, wz_s, wz_r, red_s, red_r,
):
    leaf, x, col = lax.axis_index("leaf"), lax.axis_index("row"), lax.axis_index("col")
    h, c = lax.div(leaf, 2), lax.rem(leaf, 2)
    u, z = lax.div(col, NZ), lax.rem(col, NZ)
    y = h * NU + u
    sgn = 1 - 2 * c

    def at_z(zz):
        return (leaf, x, u * NZ + zz)

    def at_u(uu):
        return (leaf, x, uu * NZ + z)

    def at_x(xx):
        return (leaf, xx, col)

    def at_y(yy, core):
        return (lax.div(yy, NU) * 2 + core, x, lax.rem(yy, NU) * NZ + z)

    def zmod(v):
        return lax.rem(v + 2 * NZ, NZ)

    def xmod(v):
        return lax.rem(v + 2 * NX, NX)

    def umod(v):
        return lax.rem(v + 2 * NU, NU)

    started = []

    def send(src, dst, ssem, rsem, to):
        copy = pltpu.make_async_remote_copy(
            src_ref=src, dst_ref=dst, send_sem=ssem, recv_sem=rsem, device_id=to, device_id_type=MESH
        )
        copy.start()
        started.append(copy)

    def settle():
        while started:
            started.pop(0).wait_send()

    def arrived(dst, rsem):
        pltpu.make_async_remote_copy(
            src_ref=dst, dst_ref=dst, send_sem=rsem, recv_sem=rsem, device_id=at_z(zmod(z + 1)), device_id_type=MESH
        ).wait_recv()

    barrier = pltpu.get_barrier_semaphore()
    v_copy = pltpu.make_async_copy(v_hbm.at[0], v_in, in_sem.at[0])
    v_copy.start()
    peers = [at_y(lax.rem(y + d, 8), core) for d in (1, 2, 6, 7) for core in range(2)]
    peers += [at_z(zmod(z + d)) for d in (1, 2, 6, 7)]
    peers += [at_x(xmod(x + 1)), at_x(xmod(x - 1)), (h * 2 + 1 - c, x, col)]
    for peer in peers:
        pl.semaphore_signal(barrier, inc=1, device_id=peer, device_id_type=MESH)
    outer = jnp.logical_or(u == 0, u == NU - 1)

    @pl.when(outer)
    def _():
        pl.semaphore_signal(barrier, inc=1, device_id=at_u(NU - 1 - u), device_id_type=MESH)

    half = pl.ds(pl.multiple_of(c * 64, 64), 64)
    quarter = pl.ds(pl.multiple_of(c * 32, 32), 32)
    loads = [
        pltpu.make_async_copy(f_hbm.at[:, half], f_in, in_sem.at[1]),
        pltpu.make_async_copy(f_hbm.at[h, half], fg.at[x, u, c], in_sem.at[2]),
        pltpu.make_async_copy(r_hbm, r_in, in_sem.at[3]),
        pltpu.make_async_copy(l_hbm.at[:, quarter], l_in, in_sem.at[4]),
        pltpu.make_async_copy(l_hbm.at[h, quarter], lg.at[x, u, c], in_sem.at[5]),
        pltpu.make_async_copy(loc_hbm, loc_in, in_sem.at[6]),
        pltpu.make_async_copy(map_hbm, map_in, in_sem.at[7]),
    ]
    for copy in loads:
        copy.start()
    v_copy.wait()
    vs[...] = jnp.transpose(v_in[...].astype(F32)).astype(BF16).reshape(NU, SUB, BLK)
    vall[z, u] = vs[u]
    pl.semaphore_wait(barrier, len(peers) + outer.astype(jnp.int32))

    for d in range(1, NU):
        to = umod(u + d)
        send(vs.at[to], vall.at[z, u], vsc_s.at[d], vsc_r.at[d], at_u(to))
    for copy in loads:
        copy.wait()
    xa, xb, xo = xmod(x + sgn), xmod(x - sgn), xmod(x + 2)
    y_steps = [sgn, -sgn, 2 * sgn]
    for i, step in enumerate(y_steps):
        yy = lax.rem(y + step + 16, 8)
        send(f_in.at[lax.div(yy, NU)], fg.at[x, u, c], fy_s.at[i], fy_r.at[i], at_y(yy, c))
    u_from = [u] + [umod(u - step) for step in y_steps]

    def f_x_first(i):
        if i > 0:
            arrived(fg.at[x, u_from[i], c], fy_r.at[i - 1])
        if i == 3:
            send(fg.at[x, u_from[i], c], fg.at[x, u_from[i], c], fx_s.at[i, 2], fx_r.at[i, 2], at_x(xo))
        send(fg.at[x, u_from[i], c], fg.at[x, u_from[i], c], fx_s.at[i, 0], fx_r.at[i, 0], at_x(xa))
        send(fg.at[x, u_from[i], c], fg.at[x, u_from[i], c], fx_s.at[i, 1], fx_r.at[i, 1], at_x(xb))

    def f_x_second(i):
        if i != 3:
            arrived(fg.at[xb, u_from[i], c], fx_r.at[i, 0])
            send(fg.at[xb, u_from[i], c], fg.at[xb, u_from[i], c], fx_s.at[i, 2], fx_r.at[i, 2], at_x(xa))

    def z_first(array, part, ssem, rsem, way):
        block = array.at[z, part]
        send(block, block, ssem.at[2], rsem.at[2], at_z(zmod(z + 2 * way)))
        send(block, block, ssem.at[1], rsem.at[1], at_z(zmod(z + way)))

    def z_second(array, part, ssem, rsem, way, last):
        block = array.at[zmod(z - 2 * way), part]
        arrived(block, rsem.at[2])
        if last == 4:
            send(block, block, ssem.at[4], rsem.at[4], at_z(zmod(z + 2 * way)))
        send(block, block, ssem.at[3], rsem.at[3], at_z(zmod(z + way)))

    def z_last(array, part, rsem, way, numbers):
        for number in numbers:
            arrived(array.at[zmod(z - number * way), part], rsem.at[number])

    v_parts = [pl.ds(umod(u - d), 1) for d in range(NU)]

    def v_first(d):
        if d:
            arrived(vall.at[z, umod(u - d)], vsc_r.at[d])
        for number, way in ((2 * d, sgn), (2 * d + 1, -sgn)):
            z_first(vall, v_parts[d], vz_s.at[number], vz_r.at[number], way)

    def v_second(d):
        z_second(vall, v_parts[d], vz_s.at[2 * d], vz_r.at[2 * d], sgn, 4)
        z_second(vall, v_parts[d], vz_s.at[2 * d + 1], vz_r.at[2 * d + 1], -sgn, 3)

    def v_last():
        for d in range(NU):
            z_last(vall, v_parts[d], vz_r.at[2 * d], sgn, (1, 3, 4))
            z_last(vall, v_parts[d], vz_r.at[2 * d + 1], -sgn, (1, 3))

    sibling = (h * 2 + 1 - c, x, col)

    def to_sibling(array, xx, i, ssem, rsem):
        send(array.at[xx, :, c], array.at[xx, :, c], ssem.at[i], rsem.at[i], sibling)

    def from_sibling(array, rsem, places):
        for i, xx in enumerate(places):
            arrived(array.at[xx, :, 1 - c], rsem.at[i])

    def bulk_x_first(array, ssem, rsem):
        send(array.at[x, :, c], array.at[x, :, c], ssem.at[0], rsem.at[0], at_x(xa))
        send(array.at[x, :, c], array.at[x, :, c], ssem.at[1], rsem.at[1], at_x(xb))

    def bulk_x_second(array, ssem, rsem):
        arrived(array.at[xb, :, c], rsem.at[0])
        send(array.at[xb, :, c], array.at[xb, :, c], ssem.at[2], rsem.at[2], at_x(xa))

    v_first(0)
    f_x_first(0)
    v_first(1)
    v_first(3)
    v_first(2)
    f_x_first(1)
    f_x_first(2)
    v_second(0)
    f_x_second(0)
    f_x_first(3)
    to_sibling(fg, x, 0, fd_s, fd_r)
    target = leaf
    r_sends = []
    for t in range(2):
        for core in range(2):
            rows = r_in.at[pl.ds(core * 64, 64)]
            place = rg.at[x, u, core]
            mine = jnp.logical_and(jnp.logical_and(h == t, c == core), u == target)
            copy = pltpu.make_async_remote_copy(
                src_ref=rows, dst_ref=place, send_sem=ry_s.at[t * 2 + core], recv_sem=ry_r.at[u],
                device_id=(2 * t + core, x, target * NZ + z), device_id_type=MESH,
            )
            r_sends.append((mine, copy))

            @pl.when(mine)
            def _():
                pltpu.make_async_copy(rows, place, ry_r.at[u]).start()

            @pl.when(jnp.logical_not(mine))
            def _():
                copy.start()
    for i, step in enumerate(y_steps):
        yy = lax.rem(y + step + 16, 8)
        send(l_in.at[lax.div(yy, NU)], lg.at[x, u, c], ly_s.at[i], ly_r.at[i], at_y(yy, c))
    v_second(1)
    v_second(3)
    f_x_second(1)
    f_x_second(2)
    v_second(2)
    f_x_second(3)
    arrived(fg.at[xb, u_from[3], c], fx_r.at[3, 0])
    to_sibling(fg, xb, 1, fd_s, fd_r)
    for i in range(4):
        arrived(fg.at[xa, u_from[i], c], fx_r.at[i, 1])
    to_sibling(fg, xa, 2, fd_s, fd_r)
    for i in range(4):
        block = fg.at[xo, u_from[i], c]
        arrived(block, fx_r.at[i, 2])
        send(block, block, fd_s.at[3 + i], fd_r.at[3 + i], sibling)
    for i in range(4):
        arrived(rg.at[x, i, c], ry_r.at[i])
    bulk_x_first(rg, rx_s, rx_r)
    for i in range(1, 4):
        arrived(lg.at[x, u_from[i], c], ly_r.at[i - 1])
    bulk_x_first(lg, lx_s, lx_r)
    v_last()
    from_sibling(fg, fd_r, (x, xa, xb))
    for i, uu in enumerate([u] + [umod(u + step) for step in y_steps]):
        arrived(fg.at[xo, uu, 1 - c], fd_r.at[3 + i])

    def p_chunk(xx):
        return jnp.concatenate([vall[4 * (xx % 2) + i, 2 + xx // 2] for i in range(4)], axis=1)

    for pair in range(2):
        total = jnp.zeros((SUB, 256), F32)
        for xx in range(NX):
            total += dot_nt(p_chunk(xx), fg[xx, 2 * pair:2 * pair + 2].reshape(256, 512))
        acc[pair] = total
    for b in range(NU):
        block = b * NZ + z
        slot = jnp.int32(0)
        present = jnp.int32(0)
        for k in range(SLOTS):
            hit = map_in[leaf, k] == block
            slot = jnp.where(hit, k, slot)
            present = jnp.where(hit, 1, present)
        padded = vall[lax.rem(slot, NZ), lax.div(slot, NZ)].astype(F32) * present.astype(F32)
        wm[u, b] = (padded - acc[b // 2, :, (b % 2) * BLK:(b % 2 + 1) * BLK]).astype(BF16)

    pltpu.make_async_copy(wm.at[u, u], wk.at[z, u], wc_r.at[0]).start()
    for d in range(1, NU):
        to = umod(u + d)
        send(wm.at[u, to], wk.at[z, u], wc_s.at[d], wc_r.at[d], at_u(to))
    order = (0, 1, 3, 2)
    parts = [pl.ds(umod(u - d), 1) for d in order]
    for k in range(NU):
        arrived(wk.at[z, parts[k]], wc_r.at[order[k]])
        z_first(wk, parts[k], wz_s.at[k], wz_r.at[k], -sgn)
    for d in range(1, NU):
        to = umod(u + d)
        for i in range(1, NU):
            rows = wm.at[u, umod(to + i)]
            send(rows, rows, wf_s.at[d, i], wf_r.at[d, i], at_u(to))
    for d in range(1, NU):
        wm[umod(u - d), u] = wk[z, umod(u - d)]
    for array, xs, xr, ds, dr in ((rg, rx_s, rx_r, rd_s, rd_r), (lg, lx_s, lx_r, ld_s, ld_r)):
        bulk_x_second(array, xs, xr)
        to_sibling(array, x, 0, ds, dr)
        to_sibling(array, xb, 1, ds, dr)
        arrived(array.at[xa, :, c], xr.at[1])
        to_sibling(array, xa, 2, ds, dr)
    for k in range(NU):
        z_second(wk, parts[k], wz_s.at[k], wz_r.at[k], -sgn, 4)
    for array, xr, ds, dr in ((rg, rx_r, rd_s, rd_r), (lg, lx_r, ld_s, ld_r)):
        arrived(array.at[xo, :, c], xr.at[2])
        to_sibling(array, xo, 3, ds, dr)

    from_sibling(lg, ld_r, (x, xa, xb, xo))
    total = jnp.zeros((SUB, 256), F32)
    for xx in range(NX):
        total += dot_nt(p_chunk(xx), lg[xx].reshape(256, 512))
    lane = lax.broadcasted_iota(jnp.int32, (SUB, BLK), 1)
    odd = lax.rem(z, 2).astype(F32)
    l_sum = jnp.zeros((SUB, BLK), F32)
    for pair in range(2):
        one, two = (vall[4 * i + lax.div(z, 2), 2 + pair].astype(F32) for i in range(2))
        one_turned, two_turned = pltpu.roll(one, 64, 1), pltpu.roll(two, 64, 1)
        rows = jnp.where(
            lane < 64, one_turned * odd + one * (1.0 - odd), two * odd + two_turned * (1.0 - odd)
        )
        l_sum += rows * total[:, pair * BLK:(pair + 1) * BLK]
    l_acc[...] = l_sum
    from_sibling(rg, rd_r, (x, xa, xb, xo))
    settle()

    def w_rows(d):
        block = wk[zmod(z + sgn * d)].reshape(NU * SUB, BLK)
        return block * 2 if 1 <= d <= 3 else block

    def r_block(pair, d):
        zz = zmod(z + sgn * d)
        lanes = pl.ds(pl.multiple_of(lax.rem(zz, 2) * BLK, BLK), BLK)
        return rg[lax.div(zz, 2), 2 * pair:2 * pair + 2, :, :, lanes].reshape(256, BLK)

    for k in range(NU):
        z_last(wk, parts[k], wz_r.at[k], -sgn, (1, 3))
    left = jnp.concatenate([w_rows(d) for d in range(4)], axis=1)
    for pair in range(2):
        zacc[pair] = dot_nt(left, jnp.concatenate([r_block(pair, d) for d in range(4)], axis=1))
    for d in range(1, NU):
        for i in range(1, NU):
            arrived(wm.at[umod(u - d), umod(u + i)], wf_r.at[d, i])
    for k in range(NU):
        z_last(wk, parts[k], wz_r.at[k], -sgn, (4,))
    part = jnp.zeros((NU * SUB, BLK), F32)
    for pair in range(2):
        term = zacc[pair] + dot_nt(w_rows(4), r_block(pair, 4))
        for i in range(2):
            rows = wm[:, 2 * pair + i].reshape(NU * SUB, BLK).astype(F32)
            part += rows * term[:, i * BLK:(i + 1) * BLK]
    sums[...] = part
    own_rows = pl.ds(pl.multiple_of(u * SUB, SUB), SUB)
    sums[own_rows, :] = sums[own_rows, :] + l_acc[...]
    flat = jnp.sum(jnp.transpose(sums[...]), axis=0, keepdims=True)
    me = z * NU + u
    red[me] = flat
    others = [i + (i >= me).astype(jnp.int32) for i in range(NZ * NU - 1)]
    for i, other in enumerate(others):
        to = (leaf, x, lax.rem(other, NU) * NZ + lax.div(other, NU))
        send(red.at[me], red.at[me], red_s.at[i], red_r.at[me], to)
    for other in others:
        arrived(red.at[other], red_r.at[other])
    out_ref[...] = loc_in[...] + jnp.sum(red[...], axis=0)

    settle()
    for mine, copy in r_sends:
        @pl.when(jnp.logical_not(mine))
        def _():
            copy.wait_send()


def local(root_inverse, factor_first, local_first, factor_second, local_second, ancestor_map):
    dma = pltpu.SemaphoreType.DMA
    scratch = [
        pltpu.VMEM(root_inverse.shape, BF16),
        pltpu.VMEM((2, 64, 512), BF16),
        pltpu.VMEM((2, 32, 512), BF16),
        pltpu.VMEM(factor_second.shape[1:], BF16),
        pltpu.VMEM(local_second.shape, F32),
        pltpu.SMEM(ancestor_map.shape, jnp.int32),
        pltpu.VMEM((NU, SUB, BLK), BF16),
        pltpu.VMEM((NZ, NU, SUB, BLK), BF16),
        pltpu.VMEM((NX, NU, 2, 64, 512), BF16),
        pltpu.VMEM((NX, NU, 2, 32, 512), BF16),
        pltpu.VMEM((NX, NU, 2, 64, 256), BF16),
        pltpu.VMEM((NZ, NU, SUB, BLK), BF16),
        pltpu.VMEM((NU, NU, SUB, BLK), BF16),
        pltpu.VMEM((2, SUB, 256), F32),
        pltpu.VMEM((2, NU * SUB, 256), F32),
        pltpu.VMEM((NU * SUB, BLK), F32),
        pltpu.VMEM((SUB, BLK), F32),
        pltpu.VMEM((NZ * NU, 1, NU * SUB), F32),
        dma((8,)),
    ]
    for count in ((4,), (8, 5), (3,), (4, 3), (7,), (3,), (3,), (4,), (4,), (3,), (4,), (4,), (4, 4), (4, 5), (32,)):
        scratch += [dma(count), dma(count)]
    return pl.pallas_call(
        kernel,
        out_shape=jax.ShapeDtypeStruct(local_second.shape, F32),
        in_specs=[pl.BlockSpec(memory_space=pltpu.HBM)] * 6,
        out_specs=pl.BlockSpec(memory_space=pltpu.VMEM),
        scratch_shapes=scratch,
        compiler_params=pltpu.CompilerParams(
            collective_id=0, has_side_effects=True, vmem_limit_bytes=65_000_000
        ),
        name="variances",
    )(root_inverse, factor_first, local_first, factor_second, local_second, ancestor_map)


def solution(mesh):
    placed = (
        P("col", ("leaf", "row")),
        P(None, "col", "row"),
        P(None, "col", "row"),
        P("leaf", "col", "row"),
        P("leaf", "row"),
        P(),
    )
    return jax.shard_map(
        local, mesh=mesh, in_specs=placed, out_specs=P("leaf", "row"), check_vma=False
    )
```

```python
import jax
import jax.numpy as jnp
from jax import lax
from jax.experimental import pallas as pl
from jax.experimental.pallas import tpu as pltpu
from jax.sharding import PartitionSpec as P

NX, NU, NZ = 4, 4, 8
BLK = 128
SUB = 96
SLOTS = 16
MESH = pl.DeviceIdType.MESH
BF16, F32 = jnp.bfloat16, jnp.float32
NT = (((1,), (1,)), ((), ()))


def dot_nt(a, b):
    return lax.dot_general(a, b, NT, preferred_element_type=F32)


def kernel(
    r_hbm, f_hbm, l_hbm, v_hbm, loc_hbm, map_hbm, out_ref,
    r_in, f_in, l_in, v_in, loc_in, map_in,
    vs, vall, fg, lg, rg, wk, wm, acc, zacc, sums, l_acc, red,
    in_sem, vsc_s, vsc_r, vz_s, vz_r, fy_s, fy_r, fx_s, fx_r, fd_s, fd_r,
    ly_s, ly_r, lx_s, lx_r, ld_s, ld_r, ry_s, ry_r, rx_s, rx_r, rd_s, rd_r,
    wc_s, wc_r, wf_s, wf_r, wz_s, wz_r, red_s, red_r,
):
    leaf, x, col = lax.axis_index("leaf"), lax.axis_index("row"), lax.axis_index("col")
    h, c = lax.div(leaf, 2), lax.rem(leaf, 2)
    u, z = lax.div(col, NZ), lax.rem(col, NZ)
    y = h * NU + u
    sgn = 1 - 2 * c

    def at_z(zz):
        return (leaf, x, u * NZ + zz)

    def at_u(uu):
        return (leaf, x, uu * NZ + z)

    def at_x(xx):
        return (leaf, xx, col)

    def at_y(yy, core):
        return (lax.div(yy, NU) * 2 + core, x, lax.rem(yy, NU) * NZ + z)

    def zmod(v):
        return lax.rem(v + 2 * NZ, NZ)

    def xmod(v):
        return lax.rem(v + 2 * NX, NX)

    def umod(v):
        return lax.rem(v + 2 * NU, NU)

    started = []

    def send(src, dst, ssem, rsem, to):
        copy = pltpu.make_async_remote_copy(
            src_ref=src, dst_ref=dst, send_sem=ssem, recv_sem=rsem, device_id=to, device_id_type=MESH
        )
        copy.start()
        started.append(copy)

    def settle():
        while started:
            started.pop(0).wait_send()

    def arrived(dst, rsem):
        pltpu.make_async_remote_copy(
            src_ref=dst, dst_ref=dst, send_sem=rsem, recv_sem=rsem, device_id=at_z(zmod(z + 1)), device_id_type=MESH
        ).wait_recv()

    barrier = pltpu.get_barrier_semaphore()
    v_copy = pltpu.make_async_copy(v_hbm.at[0], v_in, in_sem.at[0])
    v_copy.start()
    peers = [at_y(lax.rem(y + d, 8), core) for d in (1, 2, 6, 7) for core in range(2)]
    peers += [at_z(zmod(z + d)) for d in (1, 2, 6, 7)]
    peers += [at_x(xmod(x + 1)), at_x(xmod(x - 1)), (h * 2 + 1 - c, x, col)]
    for peer in peers:
        pl.semaphore_signal(barrier, inc=1, device_id=peer, device_id_type=MESH)
    outer = jnp.logical_or(u == 0, u == NU - 1)

    @pl.when(outer)
    def _():
        pl.semaphore_signal(barrier, inc=1, device_id=at_u(NU - 1 - u), device_id_type=MESH)

    half = pl.ds(pl.multiple_of(c * 64, 64), 64)
    quarter = pl.ds(pl.multiple_of(c * 32, 32), 32)
    loads = [
        pltpu.make_async_copy(f_hbm.at[:, half], f_in, in_sem.at[1]),
        pltpu.make_async_copy(f_hbm.at[h, half], fg.at[x, u, c], in_sem.at[2]),
        pltpu.make_async_copy(r_hbm, r_in, in_sem.at[3]),
        pltpu.make_async_copy(l_hbm.at[:, quarter], l_in, in_sem.at[4]),
        pltpu.make_async_copy(l_hbm.at[h, quarter], lg.at[x, u, c], in_sem.at[5]),
        pltpu.make_async_copy(loc_hbm, loc_in, in_sem.at[6]),
        pltpu.make_async_copy(map_hbm, map_in, in_sem.at[7]),
    ]
    for copy in loads:
        copy.start()
    v_copy.wait()
    vs[...] = jnp.transpose(v_in[...].astype(F32)).astype(BF16).reshape(NU, SUB, BLK)
    vall[z, u] = vs[u]
    pl.semaphore_wait(barrier, len(peers) + outer.astype(jnp.int32))

    for d in range(1, NU):
        to = umod(u + d)
        send(vs.at[to], vall.at[z, u], vsc_s.at[d], vsc_r.at[d], at_u(to))
    for copy in loads:
        copy.wait()
    xa, xb, xo = xmod(x + sgn), xmod(x - sgn), xmod(x + 2)
    y_steps = [sgn, -sgn, 2 * sgn]
    for i, step in enumerate(y_steps):
        yy = lax.rem(y + step + 16, 8)
        send(f_in.at[lax.div(yy, NU)], fg.at[x, u, c], fy_s.at[i], fy_r.at[i], at_y(yy, c))
    u_from = [u] + [umod(u - step) for step in y_steps]

    def f_x_first(i):
        if i > 0:
            arrived(fg.at[x, u_from[i], c], fy_r.at[i - 1])
        if i == 3:
            send(fg.at[x, u_from[i], c], fg.at[x, u_from[i], c], fx_s.at[i, 2], fx_r.at[i, 2], at_x(xo))
        send(fg.at[x, u_from[i], c], fg.at[x, u_from[i], c], fx_s.at[i, 0], fx_r.at[i, 0], at_x(xa))
        send(fg.at[x, u_from[i], c], fg.at[x, u_from[i], c], fx_s.at[i, 1], fx_r.at[i, 1], at_x(xb))

    def f_x_second(i):
        if i != 3:
            arrived(fg.at[xb, u_from[i], c], fx_r.at[i, 0])
            send(fg.at[xb, u_from[i], c], fg.at[xb, u_from[i], c], fx_s.at[i, 2], fx_r.at[i, 2], at_x(xa))

    def z_first(array, part, ssem, rsem, way):
        block = array.at[z, part]
        send(block, block, ssem.at[2], rsem.at[2], at_z(zmod(z + 2 * way)))
        send(block, block, ssem.at[1], rsem.at[1], at_z(zmod(z + way)))

    def z_second(array, part, ssem, rsem, way, last):
        block = array.at[zmod(z - 2 * way), part]
        arrived(block, rsem.at[2])
        if last == 4:
            send(block, block, ssem.at[4], rsem.at[4], at_z(zmod(z + 2 * way)))
        send(block, block, ssem.at[3], rsem.at[3], at_z(zmod(z + way)))

    def z_last(array, part, rsem, way, numbers):
        for number in numbers:
            arrived(array.at[zmod(z - number * way), part], rsem.at[number])

    v_parts = [pl.ds(umod(u - d), 1) for d in range(NU)]

    def v_first(d):
        if d:
            arrived(vall.at[z, umod(u - d)], vsc_r.at[d])
        for number, way in ((2 * d, sgn), (2 * d + 1, -sgn)):
            z_first(vall, v_parts[d], vz_s.at[number], vz_r.at[number], way)

    def v_second(d):
        z_second(vall, v_parts[d], vz_s.at[2 * d], vz_r.at[2 * d], sgn, 4)
        z_second(vall, v_parts[d], vz_s.at[2 * d + 1], vz_r.at[2 * d + 1], -sgn, 3)

    def v_last():
        for d in range(NU):
            z_last(vall, v_parts[d], vz_r.at[2 * d], sgn, (1, 3, 4))
            z_last(vall, v_parts[d], vz_r.at[2 * d + 1], -sgn, (1, 3))

    sibling = (h * 2 + 1 - c, x, col)

    def to_sibling(array, xx, i, ssem, rsem):
        send(array.at[xx, :, c], array.at[xx, :, c], ssem.at[i], rsem.at[i], sibling)

    def from_sibling(array, rsem, places):
        for i, xx in enumerate(places):
            arrived(array.at[xx, :, 1 - c], rsem.at[i])

    def bulk_x_first(array, ssem, rsem):
        send(array.at[x, :, c], array.at[x, :, c], ssem.at[0], rsem.at[0], at_x(xa))
        send(array.at[x, :, c], array.at[x, :, c], ssem.at[1], rsem.at[1], at_x(xb))

    def bulk_x_second(array, ssem, rsem):
        arrived(array.at[xb, :, c], rsem.at[0])
        send(array.at[xb, :, c], array.at[xb, :, c], ssem.at[2], rsem.at[2], at_x(xa))

    v_first(0)
    f_x_first(0)
    v_first(1)
    v_first(3)
    v_first(2)
    f_x_first(1)
    f_x_first(2)
    v_second(0)
    f_x_second(0)
    f_x_first(3)
    to_sibling(fg, x, 0, fd_s, fd_r)
    target = leaf
    r_sends = []
    for t in range(2):
        for core in range(2):
            rows = r_in.at[pl.ds(core * 64, 64)]
            place = rg.at[x, u, core]
            mine = jnp.logical_and(jnp.logical_and(h == t, c == core), u == target)
            copy = pltpu.make_async_remote_copy(
                src_ref=rows, dst_ref=place, send_sem=ry_s.at[t * 2 + core], recv_sem=ry_r.at[u],
                device_id=(2 * t + core, x, target * NZ + z), device_id_type=MESH,
            )
            r_sends.append((mine, copy))

            @pl.when(mine)
            def _():
                pltpu.make_async_copy(rows, place, ry_r.at[u]).start()

            @pl.when(jnp.logical_not(mine))
            def _():
                copy.start()
    for i, step in enumerate(y_steps):
        yy = lax.rem(y + step + 16, 8)
        send(l_in.at[lax.div(yy, NU)], lg.at[x, u, c], ly_s.at[i], ly_r.at[i], at_y(yy, c))
    v_second(1)
    v_second(3)
    f_x_second(1)
    f_x_second(2)
    v_second(2)
    f_x_second(3)
    arrived(fg.at[xb, u_from[3], c], fx_r.at[3, 0])
    to_sibling(fg, xb, 1, fd_s, fd_r)
    for i in range(4):
        arrived(fg.at[xa, u_from[i], c], fx_r.at[i, 1])
    to_sibling(fg, xa, 2, fd_s, fd_r)
    for i in range(4):
        block = fg.at[xo, u_from[i], c]
        arrived(block, fx_r.at[i, 2])
        send(block, block, fd_s.at[3 + i], fd_r.at[3 + i], sibling)
    for i in range(4):
        arrived(rg.at[x, i, c], ry_r.at[i])
    bulk_x_first(rg, rx_s, rx_r)
    for i in range(1, 4):
        arrived(lg.at[x, u_from[i], c], ly_r.at[i - 1])
    bulk_x_first(lg, lx_s, lx_r)
    v_last()
    from_sibling(fg, fd_r, (x, xa, xb))
    for i, uu in enumerate([u] + [umod(u + step) for step in y_steps]):
        arrived(fg.at[xo, uu, 1 - c], fd_r.at[3 + i])

    def p_chunk(xx):
        return jnp.concatenate([vall[4 * (xx % 2) + i, 2 + xx // 2] for i in range(4)], axis=1)

    for pair in range(2):
        total = jnp.zeros((SUB, 256), F32)
        for xx in range(NX):
            total += dot_nt(p_chunk(xx), fg[xx, 2 * pair:2 * pair + 2].reshape(256, 512))
        acc[pair] = total
    for b in range(NU):
        block = b * NZ + z
        slot = jnp.int32(0)
        present = jnp.int32(0)
        for k in range(SLOTS):
            hit = map_in[leaf, k] == block
            slot = jnp.where(hit, k, slot)
            present = jnp.where(hit, 1, present)
        padded = vall[lax.rem(slot, NZ), lax.div(slot, NZ)].astype(F32) * present.astype(F32)
        wm[u, b] = (padded - acc[b // 2, :, (b % 2) * BLK:(b % 2 + 1) * BLK]).astype(BF16)

    pltpu.make_async_copy(wm.at[u, u], wk.at[z, u], wc_r.at[0]).start()
    for d in range(1, NU):
        to = umod(u + d)
        send(wm.at[u, to], wk.at[z, u], wc_s.at[d], wc_r.at[d], at_u(to))
    order = (0, 1, 3, 2)
    parts = [pl.ds(umod(u - d), 1) for d in order]
    for k in range(NU):
        arrived(wk.at[z, parts[k]], wc_r.at[order[k]])
        z_first(wk, parts[k], wz_s.at[k], wz_r.at[k], -sgn)
    for d in range(1, NU):
        to = umod(u + d)
        for i in range(1, NU):
            rows = wm.at[u, umod(to + i)]
            send(rows, rows, wf_s.at[d, i], wf_r.at[d, i], at_u(to))
    for d in range(1, NU):
        wm[umod(u - d), u] = wk[z, umod(u - d)]
    for array, xs, xr, ds, dr in ((rg, rx_s, rx_r, rd_s, rd_r), (lg, lx_s, lx_r, ld_s, ld_r)):
        bulk_x_second(array, xs, xr)
        to_sibling(array, x, 0, ds, dr)
        to_sibling(array, xb, 1, ds, dr)
        arrived(array.at[xa, :, c], xr.at[1])
        to_sibling(array, xa, 2, ds, dr)
    for k in range(NU):
        z_second(wk, parts[k], wz_s.at[k], wz_r.at[k], -sgn, 4)
    for array, xr, ds, dr in ((rg, rx_r, rd_s, rd_r), (lg, lx_r, ld_s, ld_r)):
        arrived(array.at[xo, :, c], xr.at[2])
        to_sibling(array, xo, 3, ds, dr)

    from_sibling(lg, ld_r, (x, xa, xb, xo))
    total = jnp.zeros((SUB, 256), F32)
    for xx in range(NX):
        total += dot_nt(p_chunk(xx), lg[xx].reshape(256, 512))
    lane = lax.broadcasted_iota(jnp.int32, (SUB, BLK), 1)
    odd = lax.rem(z, 2).astype(F32)
    l_sum = jnp.zeros((SUB, BLK), F32)
    for pair in range(2):
        one, two = (vall[4 * i + lax.div(z, 2), 2 + pair].astype(F32) for i in range(2))
        one_turned, two_turned = pltpu.roll(one, 64, 1), pltpu.roll(two, 64, 1)
        rows = jnp.where(
            lane < 64, one_turned * odd + one * (1.0 - odd), two * odd + two_turned * (1.0 - odd)
        )
        l_sum += rows * total[:, pair * BLK:(pair + 1) * BLK]
    l_acc[...] = l_sum
    from_sibling(rg, rd_r, (x, xa, xb, xo))
    settle()

    def w_rows(d):
        block = wk[zmod(z + sgn * d)].reshape(NU * SUB, BLK)
        return block * 2 if 1 <= d <= 3 else block

    def r_block(pair, d):
        zz = zmod(z + sgn * d)
        lanes = pl.ds(pl.multiple_of(lax.rem(zz, 2) * BLK, BLK), BLK)
        return rg[lax.div(zz, 2), 2 * pair:2 * pair + 2, :, :, lanes].reshape(256, BLK)

    for k in range(NU):
        z_last(wk, parts[k], wz_r.at[k], -sgn, (1, 3))
    left = jnp.concatenate([w_rows(d) for d in range(4)], axis=1)
    for pair in range(2):
        zacc[pair] = dot_nt(left, jnp.concatenate([r_block(pair, d) for d in range(4)], axis=1))
    for d in range(1, NU):
        for i in range(1, NU):
            arrived(wm.at[umod(u - d), umod(u + i)], wf_r.at[d, i])
    def by_rows(terms):
        part = jnp.zeros((NU * SUB, BLK), F32)
        for pair in range(2):
            term = terms(pair)
            for i in range(2):
                rows = wm[:, 2 * pair + i].reshape(NU * SUB, BLK).astype(F32)
                part += rows * term[:, i * BLK:(i + 1) * BLK]
        return part

    sums[...] = by_rows(lambda pair: zacc[pair])
    own_rows = pl.ds(pl.multiple_of(u * SUB, SUB), SUB)
    sums[own_rows, :] = sums[own_rows, :] + l_acc[...]
    for k in range(NU):
        z_last(wk, parts[k], wz_r.at[k], -sgn, (4,))
    sums[...] = sums[...] + by_rows(lambda pair: dot_nt(w_rows(4), r_block(pair, 4)))
    flat = jnp.sum(jnp.transpose(sums[...]), axis=0, keepdims=True)
    me = z * NU + u
    red[me] = flat
    others = [i + (i >= me).astype(jnp.int32) for i in range(NZ * NU - 1)]
    for i, other in enumerate(others):
        to = (leaf, x, lax.rem(other, NU) * NZ + lax.div(other, NU))
        send(red.at[me], red.at[me], red_s.at[i], red_r.at[me], to)
    for other in others:
        arrived(red.at[other], red_r.at[other])
    out_ref[...] = loc_in[...] + jnp.sum(red[...], axis=0)

    settle()
    for mine, copy in r_sends:
        @pl.when(jnp.logical_not(mine))
        def _():
            copy.wait_send()


def local(root_inverse, factor_first, local_first, factor_second, local_second, ancestor_map):
    dma = pltpu.SemaphoreType.DMA
    scratch = [
        pltpu.VMEM(root_inverse.shape, BF16),
        pltpu.VMEM((2, 64, 512), BF16),
        pltpu.VMEM((2, 32, 512), BF16),
        pltpu.VMEM(factor_second.shape[1:], BF16),
        pltpu.VMEM(local_second.shape, F32),
        pltpu.SMEM(ancestor_map.shape, jnp.int32),
        pltpu.VMEM((NU, SUB, BLK), BF16),
        pltpu.VMEM((NZ, NU, SUB, BLK), BF16),
        pltpu.VMEM((NX, NU, 2, 64, 512), BF16),
        pltpu.VMEM((NX, NU, 2, 32, 512), BF16),
        pltpu.VMEM((NX, NU, 2, 64, 256), BF16),
        pltpu.VMEM((NZ, NU, SUB, BLK), BF16),
        pltpu.VMEM((NU, NU, SUB, BLK), BF16),
        pltpu.VMEM((2, SUB, 256), F32),
        pltpu.VMEM((2, NU * SUB, 256), F32),
        pltpu.VMEM((NU * SUB, BLK), F32),
        pltpu.VMEM((SUB, BLK), F32),
        pltpu.VMEM((NZ * NU, 1, NU * SUB), F32),
        dma((8,)),
    ]
    for count in ((4,), (8, 5), (3,), (4, 3), (7,), (3,), (3,), (4,), (4,), (3,), (4,), (4,), (4, 4), (4, 5), (32,)):
        scratch += [dma(count), dma(count)]
    return pl.pallas_call(
        kernel,
        out_shape=jax.ShapeDtypeStruct(local_second.shape, F32),
        in_specs=[pl.BlockSpec(memory_space=pltpu.HBM)] * 6,
        out_specs=pl.BlockSpec(memory_space=pltpu.VMEM),
        scratch_shapes=scratch,
        compiler_params=pltpu.CompilerParams(
            collective_id=0, has_side_effects=True, vmem_limit_bytes=65_000_000
        ),
        name="variances",
    )(root_inverse, factor_first, local_first, factor_second, local_second, ancestor_map)


def solution(mesh):
    placed = (
        P("col", ("leaf", "row")),
        P(None, "col", "row"),
        P(None, "col", "row"),
        P("leaf", "col", "row"),
        P("leaf", "row"),
        P(),
    )
    return jax.shard_map(
        local, mesh=mesh, in_specs=placed, out_specs=P("leaf", "row"), check_vma=False
    )
```

```python
import jax
import jax.numpy as jnp
from jax import lax
from jax.experimental import pallas as pl
from jax.experimental.pallas import tpu as pltpu
from jax.sharding import PartitionSpec as P

NX, NU, NZ = 4, 4, 8
BLK = 128
SUB = 96
SLOTS = 16
MESH = pl.DeviceIdType.MESH
BF16, F32 = jnp.bfloat16, jnp.float32
NT = (((1,), (1,)), ((), ()))


def dot_nt(a, b):
    return lax.dot_general(a, b, NT, preferred_element_type=F32)


def kernel(
    r_hbm, f_hbm, l_hbm, v_hbm, loc_hbm, map_hbm, out_ref,
    r_in, f_in, l_in, v_in, loc_in, map_in,
    vs, vall, fg, lg, rg, wk, wm, acc, zacc, sums, l_acc, red,
    in_sem, vsc_s, vsc_r, vz_s, vz_r, fy_s, fy_r, fx_s, fx_r, fd_s, fd_r,
    ly_s, ly_r, lx_s, lx_r, ld_s, ld_r, ry_s, ry_r, rx_s, rx_r, rd_s, rd_r,
    wc_s, wc_r, wf_s, wf_r, wz_s, wz_r, red_s, red_r,
):
    leaf, x, col = lax.axis_index("leaf"), lax.axis_index("row"), lax.axis_index("col")
    h, c = lax.div(leaf, 2), lax.rem(leaf, 2)
    u, z = lax.div(col, NZ), lax.rem(col, NZ)
    y = h * NU + u
    sgn = 1 - 2 * c

    def at_z(zz):
        return (leaf, x, u * NZ + zz)

    def at_u(uu):
        return (leaf, x, uu * NZ + z)

    def at_x(xx):
        return (leaf, xx, col)

    def at_y(yy, core):
        return (lax.div(yy, NU) * 2 + core, x, lax.rem(yy, NU) * NZ + z)

    def zmod(v):
        return lax.rem(v + 2 * NZ, NZ)

    def xmod(v):
        return lax.rem(v + 2 * NX, NX)

    def umod(v):
        return lax.rem(v + 2 * NU, NU)

    started = []

    def send(src, dst, ssem, rsem, to):
        copy = pltpu.make_async_remote_copy(
            src_ref=src, dst_ref=dst, send_sem=ssem, recv_sem=rsem, device_id=to, device_id_type=MESH
        )
        copy.start()
        started.append(copy)

    def settle():
        while started:
            started.pop(0).wait_send()

    def arrived(dst, rsem):
        pltpu.make_async_remote_copy(
            src_ref=dst, dst_ref=dst, send_sem=rsem, recv_sem=rsem, device_id=at_z(zmod(z + 1)), device_id_type=MESH
        ).wait_recv()

    barrier = pltpu.get_barrier_semaphore()
    v_copy = pltpu.make_async_copy(v_hbm.at[0], v_in, in_sem.at[0])
    v_copy.start()
    peers = [at_y(lax.rem(y + d, 8), core) for d in (1, 2, 6, 7) for core in range(2)]
    peers += [at_z(zmod(z + d)) for d in (1, 2, 6, 7)]
    peers += [at_x(xmod(x + 1)), at_x(xmod(x - 1)), (h * 2 + 1 - c, x, col)]
    for peer in peers:
        pl.semaphore_signal(barrier, inc=1, device_id=peer, device_id_type=MESH)
    outer = jnp.logical_or(u == 0, u == NU - 1)

    @pl.when(outer)
    def _():
        pl.semaphore_signal(barrier, inc=1, device_id=at_u(NU - 1 - u), device_id_type=MESH)

    half = pl.ds(pl.multiple_of(c * 64, 64), 64)
    quarter = pl.ds(pl.multiple_of(c * 32, 32), 32)
    loads = [
        pltpu.make_async_copy(f_hbm.at[:, half], f_in, in_sem.at[1]),
        pltpu.make_async_copy(f_hbm.at[h, half], fg.at[x, u, c], in_sem.at[2]),
        pltpu.make_async_copy(r_hbm, r_in, in_sem.at[3]),
        pltpu.make_async_copy(l_hbm.at[:, quarter], l_in, in_sem.at[4]),
        pltpu.make_async_copy(l_hbm.at[h, quarter], lg.at[x, u, c], in_sem.at[5]),
        pltpu.make_async_copy(loc_hbm, loc_in, in_sem.at[6]),
        pltpu.make_async_copy(map_hbm, map_in, in_sem.at[7]),
    ]
    for copy in loads:
        copy.start()
    v_copy.wait()
    vs[...] = jnp.transpose(v_in[...].astype(F32)).astype(BF16).reshape(NU, SUB, BLK)
    vall[z, u] = vs[u]
    pl.semaphore_wait(barrier, len(peers) + outer.astype(jnp.int32))

    for d in range(1, NU):
        to = umod(u + d)
        send(vs.at[to], vall.at[z, u], vsc_s.at[d], vsc_r.at[d], at_u(to))
    for copy in loads:
        copy.wait()
    xa, xb, xo = xmod(x + sgn), xmod(x - sgn), xmod(x + 2)
    y_steps = [sgn, -sgn, 2 * sgn]
    for i, step in enumerate(y_steps):
        yy = lax.rem(y + step + 16, 8)
        send(f_in.at[lax.div(yy, NU)], fg.at[x, u, c], fy_s.at[i], fy_r.at[i], at_y(yy, c))
    u_from = [u] + [umod(u - step) for step in y_steps]

    def f_x_first(i):
        if i > 0:
            arrived(fg.at[x, u_from[i], c], fy_r.at[i - 1])
        if i == 3:
            send(fg.at[x, u_from[i], c], fg.at[x, u_from[i], c], fx_s.at[i, 2], fx_r.at[i, 2], at_x(xo))
        send(fg.at[x, u_from[i], c], fg.at[x, u_from[i], c], fx_s.at[i, 0], fx_r.at[i, 0], at_x(xa))
        send(fg.at[x, u_from[i], c], fg.at[x, u_from[i], c], fx_s.at[i, 1], fx_r.at[i, 1], at_x(xb))

    def f_x_second(i):
        if i != 3:
            arrived(fg.at[xb, u_from[i], c], fx_r.at[i, 0])
            send(fg.at[xb, u_from[i], c], fg.at[xb, u_from[i], c], fx_s.at[i, 2], fx_r.at[i, 2], at_x(xa))

    def z_first(array, part, ssem, rsem, way):
        block = array.at[z, part]
        send(block, block, ssem.at[2], rsem.at[2], at_z(zmod(z + 2 * way)))
        send(block, block, ssem.at[1], rsem.at[1], at_z(zmod(z + way)))

    def z_second(array, part, ssem, rsem, way, last):
        block = array.at[zmod(z - 2 * way), part]
        arrived(block, rsem.at[2])
        send(block, block, ssem.at[3], rsem.at[3], at_z(zmod(z + way)))
        if last == 4:
            send(block, block, ssem.at[4], rsem.at[4], at_z(zmod(z + 2 * way)))

    def z_last(array, part, rsem, way, numbers):
        for number in numbers:
            arrived(array.at[zmod(z - number * way), part], rsem.at[number])

    v_parts = [pl.ds(umod(u - d), 1) for d in range(NU)]

    def v_first(d):
        if d:
            arrived(vall.at[z, umod(u - d)], vsc_r.at[d])
        for number, way in ((2 * d, sgn), (2 * d + 1, -sgn)):
            z_first(vall, v_parts[d], vz_s.at[number], vz_r.at[number], way)

    def v_second(d):
        z_second(vall, v_parts[d], vz_s.at[2 * d], vz_r.at[2 * d], sgn, 4)
        z_second(vall, v_parts[d], vz_s.at[2 * d + 1], vz_r.at[2 * d + 1], -sgn, 3)

    def v_last():
        for d in range(NU):
            z_last(vall, v_parts[d], vz_r.at[2 * d], sgn, (1, 3, 4))
            z_last(vall, v_parts[d], vz_r.at[2 * d + 1], -sgn, (1, 3))

    sibling = (h * 2 + 1 - c, x, col)

    def to_sibling(array, xx, i, ssem, rsem):
        send(array.at[xx, :, c], array.at[xx, :, c], ssem.at[i], rsem.at[i], sibling)

    def from_sibling(array, rsem, places):
        for i, xx in enumerate(places):
            arrived(array.at[xx, :, 1 - c], rsem.at[i])

    def bulk_x_first(array, ssem, rsem):
        send(array.at[x, :, c], array.at[x, :, c], ssem.at[0], rsem.at[0], at_x(xa))
        send(array.at[x, :, c], array.at[x, :, c], ssem.at[1], rsem.at[1], at_x(xb))

    def bulk_x_second(array, ssem, rsem):
        arrived(array.at[xb, :, c], rsem.at[0])
        send(array.at[xb, :, c], array.at[xb, :, c], ssem.at[2], rsem.at[2], at_x(xa))

    v_first(0)
    f_x_first(0)
    v_first(1)
    v_first(3)
    v_first(2)
    f_x_first(1)
    f_x_first(2)
    v_second(0)
    f_x_second(0)
    f_x_first(3)
    to_sibling(fg, x, 0, fd_s, fd_r)
    target = leaf
    r_sends = []
    for t in range(2):
        for core in range(2):
            rows = r_in.at[pl.ds(core * 64, 64)]
            place = rg.at[x, u, core]
            mine = jnp.logical_and(jnp.logical_and(h == t, c == core), u == target)
            copy = pltpu.make_async_remote_copy(
                src_ref=rows, dst_ref=place, send_sem=ry_s.at[t * 2 + core], recv_sem=ry_r.at[u],
                device_id=(2 * t + core, x, target * NZ + z), device_id_type=MESH,
            )
            r_sends.append((mine, copy))

            @pl.when(mine)
            def _():
                pltpu.make_async_copy(rows, place, ry_r.at[u]).start()

            @pl.when(jnp.logical_not(mine))
            def _():
                copy.start()
    for i, step in enumerate(y_steps):
        yy = lax.rem(y + step + 16, 8)
        send(l_in.at[lax.div(yy, NU)], lg.at[x, u, c], ly_s.at[i], ly_r.at[i], at_y(yy, c))
    v_second(1)
    v_second(3)
    f_x_second(1)
    f_x_second(2)
    v_second(2)
    f_x_second(3)
    arrived(fg.at[xb, u_from[3], c], fx_r.at[3, 0])
    to_sibling(fg, xb, 1, fd_s, fd_r)
    for i in range(4):
        arrived(fg.at[xa, u_from[i], c], fx_r.at[i, 1])
    to_sibling(fg, xa, 2, fd_s, fd_r)
    for i in range(4):
        block = fg.at[xo, u_from[i], c]
        arrived(block, fx_r.at[i, 2])
        send(block, block, fd_s.at[3 + i], fd_r.at[3 + i], sibling)
    for i in range(4):
        arrived(rg.at[x, i, c], ry_r.at[i])
    bulk_x_first(rg, rx_s, rx_r)
    for i in range(1, 4):
        arrived(lg.at[x, u_from[i], c], ly_r.at[i - 1])
    bulk_x_first(lg, lx_s, lx_r)
    v_last()
    from_sibling(fg, fd_r, (x, xa, xb))
    for i, uu in enumerate([u] + [umod(u + step) for step in y_steps]):
        arrived(fg.at[xo, uu, 1 - c], fd_r.at[3 + i])

    def p_chunk(xx):
        return jnp.concatenate([vall[4 * (xx % 2) + i, 2 + xx // 2] for i in range(4)], axis=1)

    for pair in range(2):
        total = jnp.zeros((SUB, 256), F32)
        for xx in range(NX):
            total += dot_nt(p_chunk(xx), fg[xx, 2 * pair:2 * pair + 2].reshape(256, 512))
        acc[pair] = total
    for b in range(NU):
        block = b * NZ + z
        slot = jnp.int32(0)
        present = jnp.int32(0)
        for k in range(SLOTS):
            hit = map_in[leaf, k] == block
            slot = jnp.where(hit, k, slot)
            present = jnp.where(hit, 1, present)
        padded = vall[lax.rem(slot, NZ), lax.div(slot, NZ)].astype(F32) * present.astype(F32)
        wm[u, b] = (padded - acc[b // 2, :, (b % 2) * BLK:(b % 2 + 1) * BLK]).astype(BF16)

    pltpu.make_async_copy(wm.at[u, u], wk.at[z, u], wc_r.at[0]).start()
    for d in range(1, NU):
        to = umod(u + d)
        send(wm.at[u, to], wk.at[z, u], wc_s.at[d], wc_r.at[d], at_u(to))
    order = (0, 1, 3, 2)
    parts = [pl.ds(umod(u - d), 1) for d in order]
    for k in range(NU):
        arrived(wk.at[z, parts[k]], wc_r.at[order[k]])
        z_first(wk, parts[k], wz_s.at[k], wz_r.at[k], -sgn)
    for d in range(1, NU):
        to = umod(u + d)
        for i in range(1, NU):
            rows = wm.at[u, umod(to + i)]
            send(rows, rows, wf_s.at[d, i], wf_r.at[d, i], at_u(to))
    for d in range(1, NU):
        wm[umod(u - d), u] = wk[z, umod(u - d)]
    for array, xs, xr, ds, dr in ((rg, rx_s, rx_r, rd_s, rd_r), (lg, lx_s, lx_r, ld_s, ld_r)):
        bulk_x_second(array, xs, xr)
        to_sibling(array, x, 0, ds, dr)
        to_sibling(array, xb, 1, ds, dr)
        arrived(array.at[xa, :, c], xr.at[1])
        to_sibling(array, xa, 2, ds, dr)
    for k in range(NU):
        z_second(wk, parts[k], wz_s.at[k], wz_r.at[k], -sgn, 4)
    for array, xr, ds, dr in ((rg, rx_r, rd_s, rd_r), (lg, lx_r, ld_s, ld_r)):
        arrived(array.at[xo, :, c], xr.at[2])
        to_sibling(array, xo, 3, ds, dr)

    from_sibling(lg, ld_r, (x, xa, xb, xo))
    total = jnp.zeros((SUB, 256), F32)
    for xx in range(NX):
        total += dot_nt(p_chunk(xx), lg[xx].reshape(256, 512))
    lane = lax.broadcasted_iota(jnp.int32, (SUB, BLK), 1)
    odd = lax.rem(z, 2).astype(F32)
    l_sum = jnp.zeros((SUB, BLK), F32)
    for pair in range(2):
        one, two = (vall[4 * i + lax.div(z, 2), 2 + pair].astype(F32) for i in range(2))
        one_turned, two_turned = pltpu.roll(one, 64, 1), pltpu.roll(two, 64, 1)
        rows = jnp.where(
            lane < 64, one_turned * odd + one * (1.0 - odd), two * odd + two_turned * (1.0 - odd)
        )
        l_sum += rows * total[:, pair * BLK:(pair + 1) * BLK]
    l_acc[...] = l_sum
    from_sibling(rg, rd_r, (x, xa, xb, xo))
    settle()

    def w_rows(d):
        block = wk[zmod(z + sgn * d)].reshape(NU * SUB, BLK)
        return block * 2 if 1 <= d <= 3 else block

    def r_block(pair, d):
        zz = zmod(z + sgn * d)
        lanes = pl.ds(pl.multiple_of(lax.rem(zz, 2) * BLK, BLK), BLK)
        return rg[lax.div(zz, 2), 2 * pair:2 * pair + 2, :, :, lanes].reshape(256, BLK)

    for k in range(NU):
        z_last(wk, parts[k], wz_r.at[k], -sgn, (1, 3))
    left = jnp.concatenate([w_rows(d) for d in range(4)], axis=1)
    for pair in range(2):
        zacc[pair] = dot_nt(left, jnp.concatenate([r_block(pair, d) for d in range(4)], axis=1))
    for d in range(1, NU):
        for i in range(1, NU):
            arrived(wm.at[umod(u - d), umod(u + i)], wf_r.at[d, i])
    def by_rows(terms):
        part = jnp.zeros((NU * SUB, BLK), F32)
        for pair in range(2):
            term = terms(pair)
            for i in range(2):
                rows = wm[:, 2 * pair + i].reshape(NU * SUB, BLK).astype(F32)
                part += rows * term[:, i * BLK:(i + 1) * BLK]
        return part

    sums[...] = by_rows(lambda pair: zacc[pair])
    own_rows = pl.ds(pl.multiple_of(u * SUB, SUB), SUB)
    sums[own_rows, :] = sums[own_rows, :] + l_acc[...]
    for k in range(NU):
        z_last(wk, parts[k], wz_r.at[k], -sgn, (4,))
    sums[...] = sums[...] + by_rows(lambda pair: dot_nt(w_rows(4), r_block(pair, 4)))
    flat = jnp.sum(jnp.transpose(sums[...]), axis=0, keepdims=True)
    me = z * NU + u
    red[me] = flat
    others = [i + (i >= me).astype(jnp.int32) for i in range(NZ * NU - 1)]
    for i, other in enumerate(others):
        to = (leaf, x, lax.rem(other, NU) * NZ + lax.div(other, NU))
        send(red.at[me], red.at[me], red_s.at[i], red_r.at[me], to)
    for other in others:
        arrived(red.at[other], red_r.at[other])
    out_ref[...] = loc_in[...] + jnp.sum(red[...], axis=0)

    settle()
    for mine, copy in r_sends:
        @pl.when(jnp.logical_not(mine))
        def _():
            copy.wait_send()


def local(root_inverse, factor_first, local_first, factor_second, local_second, ancestor_map):
    dma = pltpu.SemaphoreType.DMA
    scratch = [
        pltpu.VMEM(root_inverse.shape, BF16),
        pltpu.VMEM((2, 64, 512), BF16),
        pltpu.VMEM((2, 32, 512), BF16),
        pltpu.VMEM(factor_second.shape[1:], BF16),
        pltpu.VMEM(local_second.shape, F32),
        pltpu.SMEM(ancestor_map.shape, jnp.int32),
        pltpu.VMEM((NU, SUB, BLK), BF16),
        pltpu.VMEM((NZ, NU, SUB, BLK), BF16),
        pltpu.VMEM((NX, NU, 2, 64, 512), BF16),
        pltpu.VMEM((NX, NU, 2, 32, 512), BF16),
        pltpu.VMEM((NX, NU, 2, 64, 256), BF16),
        pltpu.VMEM((NZ, NU, SUB, BLK), BF16),
        pltpu.VMEM((NU, NU, SUB, BLK), BF16),
        pltpu.VMEM((2, SUB, 256), F32),
        pltpu.VMEM((2, NU * SUB, 256), F32),
        pltpu.VMEM((NU * SUB, BLK), F32),
        pltpu.VMEM((SUB, BLK), F32),
        pltpu.VMEM((NZ * NU, 1, NU * SUB), F32),
        dma((8,)),
    ]
    for count in ((4,), (8, 5), (3,), (4, 3), (7,), (3,), (3,), (4,), (4,), (3,), (4,), (4,), (4, 4), (4, 5), (32,)):
        scratch += [dma(count), dma(count)]
    return pl.pallas_call(
        kernel,
        out_shape=jax.ShapeDtypeStruct(local_second.shape, F32),
        in_specs=[pl.BlockSpec(memory_space=pltpu.HBM)] * 6,
        out_specs=pl.BlockSpec(memory_space=pltpu.VMEM),
        scratch_shapes=scratch,
        compiler_params=pltpu.CompilerParams(
            collective_id=0, has_side_effects=True, vmem_limit_bytes=65_000_000
        ),
        name="variances",
    )(root_inverse, factor_first, local_first, factor_second, local_second, ancestor_map)


def solution(mesh):
    placed = (
        P("col", ("leaf", "row")),
        P(None, "col", "row"),
        P(None, "col", "row"),
        P("leaf", "col", "row"),
        P("leaf", "row"),
        P(),
    )
    return jax.shard_map(
        local, mesh=mesh, in_specs=placed, out_specs=P("leaf", "row"), check_vma=False
    )
```
